128 devices in a mesh: fsdp: 32 (over x, z, core), seq: 4 (over y).
Axes of the slice: x: 4, y: 4, z: 4, core: 2. Of those that a mesh axis runs over, the one named last changes fastest.
Arguments:
- inputs: bfloat16 [32, 4, 256, 1152], P('fsdp', 'seq'), may hold values from -4 to 4
- qkv_spatial: bfloat16 [32, 4, 256, 3456], P('fsdp', 'seq'), may hold values from -1.5 to 1.5
- tile_list: int32 [32, 4, 4, 3], P('fsdp', 'seq'), may hold values from 0 to 3, as said below
- tile_count: int32 [32, 4, 4], P('fsdp', 'seq'), may hold values from 1 to 3
- frame_count: int32 [32], P('fsdp'), may hold values from 2 to 4, as said below
- w_out: bfloat16 [1152, 1152], P('fsdp'), may hold values from -0.375 to 0.375
- w_qkv: bfloat16 [1152, 3456], P('fsdp'), may hold values from -0.1875 to 0.1875
- cot_y: bfloat16 [32, 4, 256, 1152], P('fsdp', 'seq'), may hold values from -6 to 6
- cot_out: bfloat16 [32, 4, 256, 1152], P('fsdp', None, 'seq'), may hold values from -6 to 6
Outputs:
- resid: bfloat16 [32, 4, 256, 1152], P('fsdp', 'seq')
- temporal_out: bfloat16 [32, 4, 256, 1152], P('fsdp', None, 'seq')
- grad_inputs: bfloat16 [32, 4, 256, 1152], P('fsdp', 'seq')
- grad_qkv: bfloat16 [32, 4, 256, 3456], P('fsdp', 'seq')
- grad_w_out: float32 [1152, 1152], P('fsdp')
- grad_w_qkv: float32 [1152, 3456], P('fsdp')
The draws below stay inside these ranges and needn't reach their ends.
Inputs may be any that keep to these rules, and one draw needn't show every extreme that they name: `tile_list`: each list names 3 different tiles of the same frame. `frame_count`: frames from this count on are padding; some clip has no padding.
All inputs are finite; a program needn't handle non-finite values.
Results may differ from the reference program's by a relative error of at most 0.03.
Values may be sent and summed in bfloat16 or wider, within the bound.
No kernel may reach another device: no remote copies, remote signals or barrier semaphores. Data moves between devices by JAX's collectives and lax.ppermute only.
A program may use at most 192 MiB of HBM per device.

```python
import math
import jax
import jax.numpy as jnp
from jax import lax

D = 1152
HEADS = 16
HEAD_DIM = 72
TILE = 64
LIST_LEN = 3
TOK_FRAME = 256
FRAMES = 4
TILES = 4
CLIPS = 32


def draw_tile_list(key, part):
    key = jax.random.fold_in(key, 7)
    scores = jax.random.randint(key, (CLIPS, FRAMES, TILES, TILES), 0, 1 << 16) * TILES + jnp.arange(TILES)
    order = jnp.argsort(scores, axis=-1)
    return order[..., :LIST_LEN].astype(jnp.int32)


def draw_frame_count(key, part):
    key = jax.random.fold_in(key, 11)
    first, second = jax.random.split(key)
    counts = jax.random.randint(first, (CLIPS,), FRAMES // 2, FRAMES + 1)
    chosen = jax.random.randint(second, (), 0, CLIPS)
    return counts.at[chosen].set(FRAMES).astype(jnp.int32)


def plant(result, own_key, smallest, largest):
    longest = result.shape.index(max(result.shape))
    spots = []
    for shift in (0, 1):
        where = [jax.random.randint(jax.random.fold_in(own_key, axis), (), 0, length) for axis, length in enumerate(result.shape)]
        where[longest] = (where[longest] + shift) % result.shape[longest]
        spots.append(tuple(where))
    return result.at[spots[0]].set(smallest).at[spots[1]].set(largest)


def block_scale(key, shape, cuts, low, top_value):
    def one(axis_at, blocks):
        draws = jax.random.uniform(jax.random.fold_in(jax.random.fold_in(key, 6), axis_at), (blocks,), jnp.float32, low / len(cuts), top_value / len(cuts))
        return jnp.repeat(jnp.exp(draws), shape[axis_at] // blocks).reshape((-1,) + (1,) * (len(shape) - axis_at - 1))

    factor_of = one(*cuts[0])
    for cut in cuts[1:]:
        factor_of = factor_of * one(*cut)
    return factor_of


def bell_draw(key, shape, width, most, cuts=(), held_as=jnp.bfloat16):
    result = width * jax.random.normal(key, shape, jnp.float32)
    if cuts:
        result = result * block_scale(key, shape, cuts, -0.22, 0.18)
    return jnp.clip(result, -most, most).astype(held_as)


def setup_inputs(seed: int = 0) -> dict:
    streams_of = jax.random.split(jax.random.key(seed), 10)
    return {
        "inputs": bell_draw(streams_of[0], (CLIPS, FRAMES, TOK_FRAME, D), 0.5, 4.0, ((0, 32), (1, 4))),
        "qkv_spatial": jnp.clip(jax.random.uniform(streams_of[1], (CLIPS, FRAMES, TOK_FRAME, 3 * D), jnp.float32, -1.5, 1.5) * block_scale(streams_of[1], (CLIPS, FRAMES, TOK_FRAME, 3 * D), ((0, 32), (1, 4)), -0.4, 0.0), -1.5, 1.5).astype(jnp.bfloat16),
        "tile_list": draw_tile_list(jax.random.fold_in(streams_of[9], 71), 0),
        "tile_count": plant(jax.random.randint(streams_of[3], (CLIPS, FRAMES, TILES), 1, LIST_LEN + 1), jax.random.fold_in(streams_of[3], 1), 1, LIST_LEN).astype(jnp.int32),
        "frame_count": draw_frame_count(jax.random.fold_in(streams_of[9], 71), 0),
        "w_out": bell_draw(streams_of[5], (D, D), (D // 4) ** -0.5, 0.375, ((0, 32),)),
        "w_qkv": bell_draw(streams_of[6], (D, 3 * D), D ** -0.5, 0.1875, ((0, 32),)),
        "cot_y": bell_draw(streams_of[7], (CLIPS, FRAMES, TOK_FRAME, D), 1.0, 6.0, ((0, 32), (1, 4))),
        "cot_out": bell_draw(streams_of[8], (CLIPS, FRAMES, TOK_FRAME, D), 1.0, 6.0, ((0, 32), (2, 4))),
    }


EPS = 1e-06

def round_trip(values):
    return lax.optimization_barrier(values.astype(jnp.bfloat16)).astype(jnp.float32)

def attend(queries, keys_in, values_in, valid, scale):
    scores = jnp.einsum('...ld,...md->...lm', queries.astype(jnp.float32), keys_in.astype(jnp.float32)) * scale
    raised = jnp.exp(scores) * valid
    probs = raised / lax.optimization_barrier(jnp.sum(raised, axis=-1, keepdims=True))
    mixed = jnp.einsum('...lm,...md->...ld', round_trip(probs), values_in.astype(jnp.float32))
    return (mixed.astype(jnp.bfloat16), probs)

def attend_back(grad_out, queries, keys_in, values_in, probs, scale):
    grad_full = grad_out.astype(jnp.float32)
    grad_probs = jnp.einsum('...ld,...md->...lm', grad_full, values_in.astype(jnp.float32))
    grad_values = jnp.einsum('...lm,...ld->...md', round_trip(probs), grad_full)
    delta = lax.optimization_barrier(jnp.sum(grad_probs * probs, axis=-1, keepdims=True))
    grad_scores = round_trip(probs * (grad_probs - delta) * scale)
    grad_queries = jnp.einsum('...lm,...md->...ld', grad_scores, keys_in.astype(jnp.float32))
    grad_keys = jnp.einsum('...lm,...ld->...md', grad_scores, queries.astype(jnp.float32))
    return (grad_queries, grad_keys, grad_values)

def spatial_parts(frame_qkv, tile_list):
    parts = frame_qkv.reshape(TILES, TILE, 3, HEADS, HEAD_DIM).transpose(2, 3, 0, 1, 4)
    chosen_keys = parts[1][:, tile_list].reshape(HEADS, TILES, LIST_LEN * TILE, HEAD_DIM)
    chosen_values = parts[2][:, tile_list].reshape(HEADS, TILES, LIST_LEN * TILE, HEAD_DIM)
    return (parts[0], chosen_keys, chosen_values)

def spatial_mask(tile_count):
    live = (jnp.arange(LIST_LEN)[None, :] < tile_count[:, None]).astype(jnp.float32)
    return jnp.repeat(live, TILE, axis=1)[None, :, None, :]

def spatial_forward(frame_qkv, tile_list, tile_count):
    queries, chosen_keys, chosen_values = spatial_parts(frame_qkv, tile_list)
    mixed, probs = attend(queries, chosen_keys, chosen_values, spatial_mask(tile_count), HEAD_DIM ** (-0.5))
    return (mixed.transpose(1, 2, 0, 3).reshape(TILES * TILE, D), probs)

def spatial_back(grad_attn, frame_qkv, tile_list, probs):
    queries, chosen_keys, chosen_values = spatial_parts(frame_qkv, tile_list)
    grad_out = grad_attn.reshape(TILES, TILE, HEADS, HEAD_DIM).transpose(2, 0, 1, 3)
    grad_q, grad_k, grad_v = attend_back(grad_out, queries, chosen_keys, chosen_values, probs, HEAD_DIM ** (-0.5))

    def spread(grad_chosen):
        pieces = grad_chosen.reshape(HEADS, TILES * LIST_LEN, TILE, HEAD_DIM).transpose(1, 0, 2, 3)
        summed = jax.ops.segment_sum(pieces, tile_list.reshape(-1), num_segments=TILES)
        return summed.transpose(1, 0, 2, 3)
    grads = jnp.stack([grad_q, spread(grad_k), spread(grad_v)])
    return grads.transpose(2, 3, 0, 1, 4).reshape(TILES * TILE, 3 * D).astype(jnp.bfloat16)

def temporal_parts(block_qkv):
    frames_n = block_qkv.shape[0]
    return block_qkv.reshape(frames_n, -1, 3, HEADS, HEAD_DIM).transpose(2, 1, 3, 0, 4)

def temporal_forward(block_qkv, count):
    frames_n = block_qkv.shape[0]
    parts = temporal_parts(block_qkv)
    valid = (jnp.arange(frames_n) < count).astype(jnp.float32)
    mixed, probs = attend(parts[0], parts[1], parts[2], valid, HEAD_DIM ** (-0.5))
    return (mixed.transpose(2, 0, 1, 3).reshape(frames_n, -1, D), probs)

def temporal_back(grad_out, block_qkv, probs):
    frames_n = block_qkv.shape[0]
    parts = temporal_parts(block_qkv)
    grad_heads = grad_out.reshape(frames_n, -1, HEADS, HEAD_DIM).transpose(1, 2, 0, 3)
    grads = jnp.stack(attend_back(grad_heads, parts[0], parts[1], parts[2], probs, HEAD_DIM ** (-0.5)))
    return grads.transpose(3, 1, 0, 2, 4).reshape(frames_n, -1, 3 * D).astype(jnp.bfloat16)

def normalize(rows):
    values = rows.astype(jnp.float32)
    centered = values - lax.optimization_barrier(jnp.mean(values, axis=-1, keepdims=True))
    rstd_vals = lax.rsqrt(lax.optimization_barrier(jnp.mean(centered * centered, axis=-1, keepdims=True)) + EPS)
    return (centered * rstd_vals, rstd_vals)

def normalize_back(grad_hidden, normed, rstd_vals):
    inner = grad_hidden - lax.optimization_barrier(jnp.mean(grad_hidden, axis=-1, keepdims=True))
    inner = inner - normed * lax.optimization_barrier(jnp.mean(grad_hidden * normed, axis=-1, keepdims=True))
    return (rstd_vals * inner).astype(jnp.bfloat16)

def reference(inputs, qkv_spatial, tile_list, tile_count, frame_count, w_out, w_qkv, cot_y, cot_out):

    def per_clip(sums, pieces):
        clip_x, clip_qkv, clip_list, clip_count, clip_frames, clip_coty, clip_coto = pieces
        attn, sprobs = jax.vmap(spatial_forward)(clip_qkv, clip_list, clip_count)
        attn_rows = attn.reshape(-1, D)
        resid = (clip_x.reshape(-1, D).astype(jnp.float32) + jnp.dot(attn_rows, w_out, preferred_element_type=jnp.float32)).astype(jnp.bfloat16)
        normed, rstd_vals = normalize(resid)
        hidden = normed.astype(jnp.bfloat16)
        proj = jnp.dot(hidden, w_qkv, preferred_element_type=jnp.float32).astype(jnp.bfloat16)
        block = proj.reshape(FRAMES, TOK_FRAME, 3 * D)
        tout, tprobs = temporal_forward(block, clip_frames)
        grad_proj = temporal_back(clip_coto, block, tprobs).reshape(-1, 3 * D)
        grad_hidden = jnp.dot(grad_proj, w_qkv.T, preferred_element_type=jnp.float32)
        norm_back = normalize_back(grad_hidden, normed, rstd_vals)
        grad_x = (clip_coty.reshape(-1, D).astype(jnp.float32) + norm_back.astype(jnp.float32)).astype(jnp.bfloat16)
        grad_attn = jnp.dot(grad_x, w_out.T, preferred_element_type=jnp.float32).astype(jnp.bfloat16)
        grad_spatial = jax.vmap(spatial_back)(grad_attn.reshape(FRAMES, TOK_FRAME, D), clip_qkv, clip_list, sprobs)
        term_out = jnp.dot(attn_rows.T, grad_x, preferred_element_type=jnp.float32)
        term_qkv = jnp.dot(hidden.T, grad_proj, preferred_element_type=jnp.float32)
        shape_rows = (FRAMES, TOK_FRAME, D)
        return ((sums[0] + term_out, sums[1] + term_qkv), (resid.reshape(shape_rows), tout, grad_x.reshape(shape_rows), grad_spatial))
    start = (jnp.zeros((D, D), jnp.float32), jnp.zeros((D, 3 * D), jnp.float32))
    sums, stacked = lax.scan(per_clip, start, (inputs, qkv_spatial, tile_list, tile_count, frame_count, cot_y, cot_out))
    factor = 1.0 / math.sqrt(CLIPS * FRAMES * TOK_FRAME)
    return (stacked[0], stacked[1], stacked[2], stacked[3], sums[0] * factor, sums[1] * factor)
```

```python
import math

import jax
import jax.numpy as jnp
from jax import lax
from jax.experimental import pallas as pl
from jax.experimental.pallas import tpu as pltpu
from jax.sharding import PartitionSpec as P

D = 1152
HEADS = 16
HEAD_DIM = 72
TILE = 64
LIST_LEN = 3
HALF = D // 2
HALF_HEADS = HEADS // 2
EPS = 1e-06
SCALE = HEAD_DIM ** (-0.5)
F32 = jnp.float32
BF16 = jnp.bfloat16
VMEM = pl.BlockSpec(memory_space=pltpu.VMEM)
SMEM = pl.BlockSpec(memory_space=pltpu.SMEM)


def dot_nn(a, b):
    return lax.dot_general(a, b, (((1,), (0,)), ((), ())), preferred_element_type=F32)


def dot_nt(a, b):
    return lax.dot_general(a, b, (((1,), (1,)), ((), ())), preferred_element_type=F32)


def dot_tn(a, b):
    return lax.dot_general(a, b, (((0,), (0,)), ((), ())), preferred_element_type=F32)


def call(kernel, out_shape, operands, specs, scratch=(), limit=40, flops=0, nbytes=0):
    many = isinstance(out_shape, (list, tuple))
    return pl.pallas_call(
        kernel,
        out_shape=out_shape,
        in_specs=specs,
        out_specs=[VMEM] * len(out_shape) if many else VMEM,
        scratch_shapes=list(scratch),
        compiler_params=pltpu.CompilerParams(vmem_limit_bytes=limit << 20),
        cost_estimate=pl.CostEstimate(flops=flops, bytes_accessed=nbytes, transcendentals=0),
    )(*operands)


def head_window(head):
    low = head * HEAD_DIM
    start = low // 128 * 128
    stop = -(-(low + HEAD_DIM) // 128) * 128
    lane = lax.broadcasted_iota(jnp.int32, (1, stop - start), 1) + start
    inside = (lane >= low) & (lane < low + HEAD_DIM)
    return start, stop, inside


def key_mask(list_ref, count_ref, mask_ref):
    rows = mask_ref.shape[0]
    key_tile = lax.broadcasted_iota(jnp.int32, (TILE, rows), 1) // TILE
    for j in range(rows // TILE):
        live = jnp.zeros((TILE, rows), F32)
        for m in range(LIST_LEN):
            named = jnp.where(m < count_ref[j], list_ref[j, m], -1)
            live = jnp.where(key_tile == named, 1.0, live)
        mask_ref[j * TILE : (j + 1) * TILE, :] = live


def head_probs(qkv_ref, mask, start, stop, inside):
    queries = qkv_ref[:, start:stop]
    keys_in = jnp.where(inside, qkv_ref[:, D + start : D + stop], 0.0).astype(BF16)
    values_in = jnp.where(inside, qkv_ref[:, 2 * D + start : 2 * D + stop], 0.0).astype(BF16)
    raised = jnp.exp(dot_nt(queries, keys_in) * SCALE) * mask
    probs = raised * (1.0 / jnp.sum(raised, axis=-1, keepdims=True))
    return queries, keys_in, values_in, probs


def spatial_forward_kernel(list_ref, count_ref, qkv_ref, attn_ref, mask_ref):
    key_mask(list_ref, count_ref, mask_ref)
    attn_ref[...] = jnp.zeros_like(attn_ref)
    for head in range(HEADS):
        start, stop, inside = head_window(head)
        _, _, values_in, probs = head_probs(qkv_ref, mask_ref[...], start, stop, inside)
        mixed = dot_nn(probs.astype(BF16), values_in).astype(BF16)
        attn_ref[:, start:stop] = attn_ref[:, start:stop] + mixed


def spatial_back_kernel(list_ref, count_ref, qkv_ref, gx_ref, w_ref, out_ref, mask_ref, ga_ref):
    key_mask(list_ref, count_ref, mask_ref)
    ga_ref[...] = dot_nt(gx_ref[...], w_ref[...]).astype(BF16)
    out_ref[...] = jnp.zeros_like(out_ref)
    for head in range(HEADS):
        start, stop, inside = head_window(head)
        queries, keys_in, values_in, probs = head_probs(
            qkv_ref, mask_ref[...], start, stop, inside
        )
        grad = jnp.where(inside, ga_ref[:, start:stop], 0.0).astype(BF16)
        queries = jnp.where(inside, queries, 0.0).astype(BF16)
        grad_probs = dot_nt(grad, values_in)
        delta = jnp.sum(grad_probs * probs, axis=-1, keepdims=True)
        grad_scores = (probs * (grad_probs - delta) * SCALE).astype(BF16)
        for offset, part in (
            (0, dot_nn(grad_scores, keys_in)),
            (D, dot_tn(grad_scores, queries)),
            (2 * D, dot_tn(probs.astype(BF16), grad)),
        ):
            where = (slice(None), slice(offset + start, offset + stop))
            out_ref[where] = out_ref[where] + part.astype(BF16)


def resid_kernel(info_ref, x_ref, attn_ref, w_ref, resid_ref, *piece_refs):
    resid_ref[...] = (x_ref[...].astype(F32) + dot_nn(attn_ref[...], w_ref[...])).astype(BF16)
    n = len(piece_refs)
    for k, piece_ref in enumerate(piece_refs):
        at = lax.rem(info_ref[0] + k, n) * TILE
        piece_ref[...] = resid_ref[pl.ds(pl.multiple_of(at, TILE), TILE), :]


def normalize(rows):
    values = rows.astype(F32)
    centered = values - jnp.mean(values, axis=-1, keepdims=True)
    rstd_vals = lax.rsqrt(jnp.mean(centered * centered, axis=-1, keepdims=True) + EPS)
    return centered * rstd_vals, rstd_vals


def temporal_kernel(info_ref, count_ref, *refs):
    n = 4
    piece_refs = refs[: 2 * n]
    w_ref, cot_own_ref, cot_other_ref = refs[2 * n : 2 * n + 3]
    (tout_own_ref, tout_other_ref, hid_ref, gp_ref, gh_own_ref, gh_other_ref) = refs[
        2 * n + 3 : 2 * n + 9
    ]
    pj_ref, prod_ref, score_ref, weight_ref, wide_ref = refs[2 * n + 9 :]
    rows = TILE
    for i in range(2 * n):
        hid_ref[i * rows : (i + 1) * rows, :] = normalize(piece_refs[i][...])[0].astype(BF16)
    pj_ref[...] = dot_nn(hid_ref[...], w_ref[...]).astype(BF16)
    lane = lax.broadcasted_iota(jnp.int32, (HALF, 128), 0) // HEAD_DIM
    head = lax.broadcasted_iota(jnp.int32, (HALF, 128), 1)
    gather_heads = jnp.where(lane == head, 1.0, 0.0).astype(BF16)
    lane = lax.broadcasted_iota(jnp.int32, (128, HALF), 1) // HEAD_DIM
    head = lax.broadcasted_iota(jnp.int32, (128, HALF), 0)
    spread_heads = jnp.where(lane == head, 1.0, 0.0).astype(BF16)
    frames = [lax.rem(info_ref[0] + n - k, n) for k in range(n)]
    for clip in range(2):
        cot_ref = (cot_own_ref, cot_other_ref)[clip]
        tout_ref = (tout_own_ref, tout_other_ref)[clip]

        def part(k, which):
            at = (clip * n + k) * rows
            return pj_ref[at : at + rows, which * HALF : (which + 1) * HALF]

        queries = [part(k, 0) for k in range(n)]
        keys_in = [part(k, 1) for k in range(n)]
        values_in = [part(k, 2) for k in range(n)]
        cots = [cot_ref[frames[k]] for k in range(n)]
        for f in range(n):
            for g in range(n):
                at = (f * n + g) * rows
                prod_ref[at : at + rows, :] = queries[f] * keys_in[g]
                at += n * n * rows
                prod_ref[at : at + rows, :] = cots[f] * values_in[g]
        score_ref[...] = dot_nn(prod_ref[...], gather_heads)
        valid = [jnp.where(frames[k] < count_ref[clip], 1.0, 0.0) for k in range(n)]
        for f in range(n):
            raised, grad_probs = [], []
            for g in range(n):
                at = (f * n + g) * rows
                raised.append(jnp.exp(score_ref[at : at + rows, :] * SCALE) * valid[g])
                at += n * n * rows
                grad_probs.append(score_ref[at : at + rows, :])
            total = (raised[0] + raised[1]) + (raised[2] + raised[3])
            inverse = 1.0 / total
            probs = [r * inverse for r in raised]
            terms = [a * b for a, b in zip(grad_probs, probs)]
            delta = (terms[0] + terms[1]) + (terms[2] + terms[3])
            for g in range(n):
                at = (f * n + g) * rows
                weight_ref[at : at + rows, :] = probs[g].astype(BF16)
                at += n * n * rows
                weight_ref[at : at + rows, :] = (
                    probs[g] * (grad_probs[g] - delta) * SCALE
                ).astype(BF16)
        wide_ref[...] = dot_nn(weight_ref[...], spread_heads)

        def prob(f, g):
            at = (f * n + g) * rows
            return wide_ref[at : at + rows, :]

        def grad_score(f, g):
            at = (n * n + f * n + g) * rows
            return wide_ref[at : at + rows, :]

        for k in range(n):
            at = (clip * n + k) * rows
            out = sum(prob(k, g) * values_in[g].astype(F32) for g in range(n))
            tout_ref[frames[k]] = out.astype(BF16)
            grad_q = sum(grad_score(k, g) * keys_in[g].astype(F32) for g in range(n))
            grad_k = sum(grad_score(f, k) * queries[f].astype(F32) for f in range(n))
            grad_v = sum(prob(f, k) * cots[f].astype(F32) for f in range(n))
            gp_ref[at : at + rows, 0:HALF] = grad_q.astype(BF16)
            gp_ref[at : at + rows, HALF : 2 * HALF] = grad_k.astype(BF16)
            gp_ref[at : at + rows, 2 * HALF : 3 * HALF] = grad_v.astype(BF16)
    gh_other_ref[...] = dot_nt(gp_ref[n * rows :, :], w_ref[...]).astype(BF16)
    gh_own_ref[...] = dot_nt(gp_ref[: n * rows, :], w_ref[...])


def weight_term_kernel(left_ref, right_ref, out_ref):
    out_ref[...] = dot_tn(left_ref[...], right_ref[...]).astype(BF16)


def norm_back_kernel(*refs):
    n = 4
    piece_refs = refs[:n]
    own_ref, other_ref = refs[n : n + 2]
    for k in range(n):
        rows = slice(k * TILE, (k + 1) * TILE)
        grad_hidden = own_ref[rows, :] + other_ref[rows, :].astype(F32)
        normed, rstd_vals = normalize(piece_refs[k][...])
        inner = grad_hidden - jnp.mean(grad_hidden, axis=-1, keepdims=True)
        inner = inner - normed * jnp.mean(grad_hidden * normed, axis=-1, keepdims=True)
        refs[n + 2 + k][...] = (rstd_vals * inner).astype(BF16)


def grad_inputs_kernel(info_ref, cot_ref, *refs):
    n = 4
    out_ref, mine_ref, theirs_ref = refs[n:]
    for k in range(n):
        at = pl.multiple_of(lax.rem(info_ref[0] + k, n) * TILE, TILE)
        rows = pl.ds(at, TILE)
        out_ref[rows, :] = (cot_ref[rows, :].astype(F32) + refs[k][...].astype(F32)).astype(BF16)
    first, second = out_ref[:, :HALF], out_ref[:, HALF:]
    is_first = info_ref[1] == 0
    mine_ref[...] = jnp.where(is_first, first, second)
    theirs_ref[...] = jnp.where(is_first, second, first)


def per_device(
    inputs, qkv_spatial, tile_list, tile_count, frame_count, w_out, w_qkv, cot_y, cot_out
):
    seq_count = lax.axis_size("seq")
    fsdp_count = lax.axis_size("fsdp")
    tok_frame = inputs.shape[2]
    place = lax.axis_index("seq")
    core = lax.axis_index("fsdp") % 2
    info = jnp.stack([place, core]).astype(jnp.int32)
    pairs = [(i, i ^ 1) for i in range(fsdp_count)]
    groups = [list(range(c, fsdp_count, 2)) for c in range(2)]
    first_core = core == 0

    def swap(values):
        return lax.ppermute(values, "fsdp", pairs)

    def turn(values, k):
        return lax.ppermute(
            values, "seq", [(i, (i + k) % seq_count) for i in range(seq_count)]
        )

    def mine_theirs(first, second):
        return jnp.where(first_core, first, second), jnp.where(first_core, second, first)

    def shaped(shape, dtype=BF16):
        return jax.ShapeDtypeStruct(shape, dtype)

    def half_columns(c):
        cuts = [w_qkv[:, i * D + c * HALF : i * D + (c + 1) * HALF] for i in range(3)]
        return jnp.concatenate(cuts + [w_out[:, c * HALF : (c + 1) * HALF]], axis=1)

    mine, theirs = mine_theirs(half_columns(0), half_columns(1))
    got = swap(theirs)
    top, bottom = mine_theirs(mine, got)
    chip_rows = jnp.concatenate([top, bottom], axis=0)
    half_out = lax.all_gather(
        chip_rows[:, 3 * HALF :], "fsdp", axis=0, tiled=True, axis_index_groups=groups
    )
    half_qkv = lax.all_gather(
        chip_rows[:, : 3 * HALF], "fsdp", axis=0, tiled=True, axis_index_groups=groups
    )
    full_out = jnp.concatenate(mine_theirs(half_out, swap(half_out)), axis=1)

    cot_mine, cot_theirs = mine_theirs(cot_out[0][..., :HALF], cot_out[0][..., HALF:])
    cot_other = swap(cot_theirs)
    counts2 = jnp.concatenate([frame_count, swap(frame_count)])

    qkv = qkv_spatial.reshape(tok_frame, 3 * D)
    lists = tile_list.reshape(-1, LIST_LEN)
    counts = tile_count.reshape(-1)
    mask_scratch = pltpu.VMEM((tok_frame, tok_frame), F32)
    attn = call(
        spatial_forward_kernel,
        shaped((tok_frame, D)),
        (lists, counts, qkv),
        [SMEM, SMEM, VMEM],
        [mask_scratch],
        flops=4 * 10**9,
        nbytes=3 * 10**6,
    )
    attn_other = swap(attn)
    resid, *pieces = call(
        resid_kernel,
        [shaped((tok_frame, D))] + [shaped((TILE, D))] * seq_count,
        (info, inputs.reshape(tok_frame, D), attn, full_out),
        [SMEM, VMEM, VMEM, VMEM],
        flops=2 * 10**9,
        nbytes=4 * 10**6,
    )
    own = [pieces[0]] + [turn(pieces[k], k) for k in range(1, seq_count)]
    other = [swap(piece) for piece in own]
    wide = 2 * seq_count * seq_count * TILE
    rows = seq_count * TILE
    tout_own, tout_other, hidden, grad_proj, gh_own, gh_other = call(
        temporal_kernel,
        [
            shaped((seq_count, TILE, HALF)),
            shaped((seq_count, TILE, HALF)),
            shaped((2 * rows, D)),
            shaped((2 * rows, 3 * HALF)),
            shaped((rows, D), F32),
            shaped((rows, D)),
        ],
        (info, counts2, *own, *other, half_qkv, cot_mine, cot_other),
        [SMEM, SMEM] + [VMEM] * (2 * seq_count + 3),
        [
            pltpu.VMEM((2 * rows, 3 * HALF), BF16),
            pltpu.VMEM((wide, HALF), BF16),
            pltpu.VMEM((wide, 128), F32),
            pltpu.VMEM((wide, 128), BF16),
            pltpu.VMEM((wide, HALF), F32),
        ],
        flops=10**10,
        nbytes=10**7,
    )
    gh_got = swap(gh_other)
    tout_got = swap(tout_other)
    term_qkv = call(
        weight_term_kernel,
        shaped((D, 3 * HALF)),
        (hidden, grad_proj),
        [VMEM, VMEM],
        flops=2 * 10**9,
        nbytes=7 * 10**6,
    )
    backs = call(
        norm_back_kernel,
        [shaped((TILE, D))] * seq_count,
        (*own, gh_own, gh_got),
        [VMEM] * (seq_count + 2),
        flops=10**8,
        nbytes=3 * 10**6,
    )
    backs = [backs[0]] + [turn(backs[k], -k) for k in range(1, seq_count)]
    grad_x, gx_mine, gx_theirs = call(
        grad_inputs_kernel,
        [shaped((tok_frame, D)), shaped((tok_frame, HALF)), shaped((tok_frame, HALF))],
        (info, cot_y.reshape(tok_frame, D), *backs),
        [SMEM] + [VMEM] * (seq_count + 1),
        flops=10**7,
        nbytes=3 * 10**6,
    )
    gx_got = swap(gx_theirs)
    term_out = call(
        weight_term_kernel,
        shaped((D, HALF)),
        (jnp.concatenate([attn, attn_other], axis=0), jnp.concatenate([gx_mine, gx_got], axis=0)),
        [VMEM, VMEM],
        flops=10**9,
        nbytes=3 * 10**6,
    )
    grad_qkv = call(
        spatial_back_kernel,
        shaped((tok_frame, 3 * D)),
        (lists, counts, qkv, grad_x, full_out),
        [SMEM, SMEM] + [VMEM] * 3,
        [mask_scratch, pltpu.VMEM((tok_frame, D), BF16)],
        flops=10**10,
        nbytes=7 * 10**6,
    )

    def summed(term):
        share = lax.psum_scatter(
            term, "fsdp", scatter_dimension=0, tiled=True, axis_index_groups=groups
        )
        return lax.psum(share, "seq")

    share = jnp.concatenate([summed(term_qkv), summed(term_out)], axis=1)
    per = share.shape[0] // 2
    keep, send = mine_theirs(share[:per], share[per:])
    left, right = mine_theirs(keep, swap(send))
    factor = 1.0 / math.sqrt(fsdp_count * seq_count * tok_frame)
    left, right = left.astype(F32) * factor, right.astype(F32) * factor
    grad_w_qkv = jnp.concatenate(
        [side[:, i * HALF : (i + 1) * HALF] for i in range(3) for side in (left, right)], axis=1
    )
    grad_w_out = jnp.concatenate([left[:, 3 * HALF :], right[:, 3 * HALF :]], axis=1)
    tout = jnp.concatenate(mine_theirs(tout_own, tout_got), axis=-1)
    return (
        resid.reshape(inputs.shape),
        tout[None],
        grad_x.reshape(inputs.shape),
        grad_qkv.reshape(qkv_spatial.shape),
        grad_w_out,
        grad_w_qkv,
    )


def solution(mesh):
    placed = (
        P("fsdp", "seq", None, None),
        P("fsdp", "seq", None, None),
        P("fsdp", "seq", None, None),
        P("fsdp", "seq", None),
        P("fsdp"),
        P("fsdp", None),
        P("fsdp", None),
        P("fsdp", "seq", None, None),
        P("fsdp", None, "seq", None),
    )
    return jax.shard_map(
        per_device,
        mesh=mesh,
        in_specs=placed,
        out_specs=(
            P("fsdp", "seq", None, None),
            P("fsdp", None, "seq", None),
            P("fsdp", "seq", None, None),
            P("fsdp", "seq", None, None),
            P("fsdp", None),
            P("fsdp", None),
        ),
        check_vma=False,
    )
```

```python
import functools
import math

import jax
import jax.numpy as jnp
from jax import lax
from jax.experimental import pallas as pl
from jax.experimental.pallas import tpu as pltpu
from jax.sharding import PartitionSpec as P

D = 1152
HEADS = 16
HEAD_DIM = 72
TILE = 64
LIST_LEN = 3
HALF = D // 2
QKV_CUT = 896
OUT_CUT = 256
CHIP_ROWS = 72
EPS = 1e-06
SCALE = HEAD_DIM ** (-0.5)
F32 = jnp.float32
BF16 = jnp.bfloat16
VMEM = pl.BlockSpec(memory_space=pltpu.VMEM)
SMEM = pl.BlockSpec(memory_space=pltpu.SMEM)


def dot_nn(a, b):
    return lax.dot_general(a, b, (((1,), (0,)), ((), ())), preferred_element_type=F32)


def dot_nt(a, b):
    return lax.dot_general(a, b, (((1,), (1,)), ((), ())), preferred_element_type=F32)


def dot_tn(a, b):
    return lax.dot_general(a, b, (((0,), (0,)), ((), ())), preferred_element_type=F32)


def call(kernel, out_shape, operands, specs, scratch=(), limit=40, flops=0, nbytes=0):
    many = isinstance(out_shape, (list, tuple))
    return pl.pallas_call(
        kernel,
        out_shape=out_shape,
        in_specs=specs,
        out_specs=[VMEM] * len(out_shape) if many else VMEM,
        scratch_shapes=list(scratch),
        compiler_params=pltpu.CompilerParams(vmem_limit_bytes=limit << 20),
        cost_estimate=pl.CostEstimate(flops=flops, bytes_accessed=nbytes, transcendentals=0),
    )(*operands)


def head_window(head):
    low = head * HEAD_DIM
    start = low // 128 * 128
    stop = -(-(low + HEAD_DIM) // 128) * 128
    lane = lax.broadcasted_iota(jnp.int32, (1, stop - start), 1) + start
    inside = (lane >= low) & (lane < low + HEAD_DIM)
    return start, stop, inside


def key_mask(list_ref, count_ref, mask_ref):
    rows = mask_ref.shape[0]
    key_tile = lax.broadcasted_iota(jnp.int32, (TILE, rows), 1) // TILE
    for j in range(rows // TILE):
        live = jnp.zeros((TILE, rows), F32)
        for m in range(LIST_LEN):
            named = jnp.where(m < count_ref[j], list_ref[j, m], -1)
            live = jnp.where(key_tile == named, 1.0, live)
        mask_ref[j * TILE : (j + 1) * TILE, :] = live


def head_probs(qkv_ref, mask, start, stop, inside):
    queries = qkv_ref[:, start:stop]
    keys_in = jnp.where(inside, qkv_ref[:, D + start : D + stop], 0.0).astype(BF16)
    values_in = jnp.where(inside, qkv_ref[:, 2 * D + start : 2 * D + stop], 0.0).astype(BF16)
    raised = jnp.exp(dot_nt(queries, keys_in) * SCALE) * mask
    probs = raised * (1.0 / jnp.sum(raised, axis=-1, keepdims=True))
    return queries, keys_in, values_in, probs


def spatial_forward_kernel(list_ref, count_ref, qkv_ref, attn_ref, mask_ref):
    key_mask(list_ref, count_ref, mask_ref)
    attn_ref[...] = jnp.zeros_like(attn_ref)
    for head in range(HEADS):
        start, stop, inside = head_window(head)
        _, _, values_in, probs = head_probs(qkv_ref, mask_ref[...], start, stop, inside)
        mixed = dot_nn(probs.astype(BF16), values_in).astype(BF16)
        attn_ref[:, start:stop] = attn_ref[:, start:stop] + mixed


def spatial_back_kernel(list_ref, count_ref, qkv_ref, gx_ref, w_ref, out_ref, mask_ref, ga_ref):
    key_mask(list_ref, count_ref, mask_ref)
    ga_ref[...] = dot_nt(gx_ref[...], w_ref[...]).astype(BF16)
    out_ref[...] = jnp.zeros_like(out_ref)
    for head in range(HEADS):
        start, stop, inside = head_window(head)
        queries, keys_in, values_in, probs = head_probs(
            qkv_ref, mask_ref[...], start, stop, inside
        )
        grad = jnp.where(inside, ga_ref[:, start:stop], 0.0).astype(BF16)
        queries = jnp.where(inside, queries, 0.0).astype(BF16)
        grad_probs = dot_nt(grad, values_in)
        delta = jnp.sum(grad_probs * probs, axis=-1, keepdims=True)
        grad_scores = (probs * (grad_probs - delta) * SCALE).astype(BF16)
        for offset, part in (
            (0, dot_nn(grad_scores, keys_in)),
            (D, dot_tn(grad_scores, queries)),
            (2 * D, dot_tn(probs.astype(BF16), grad)),
        ):
            where = (slice(None), slice(offset + start, offset + stop))
            out_ref[where] = out_ref[where] + part.astype(BF16)


def resid_kernel(info_ref, x_ref, attn_ref, own_ref, other_ref, resid_ref, w_ref, *piece_refs):
    own, other = own_ref[...], other_ref[...]
    is_first = info_ref[1] == 0
    w_ref[:, :HALF] = jnp.where(is_first, own, other)
    w_ref[:, HALF:] = jnp.where(is_first, other, own)
    resid_ref[...] = (x_ref[...].astype(F32) + dot_nn(attn_ref[...], w_ref[...])).astype(BF16)
    n = len(piece_refs)
    for k, piece_ref in enumerate(piece_refs):
        at = lax.rem(info_ref[0] + k, n) * TILE
        piece_ref[...] = resid_ref[pl.ds(pl.multiple_of(at, TILE), TILE), :]


def normalize(rows):
    values = rows.astype(F32)
    centered = values - jnp.mean(values, axis=-1, keepdims=True)
    rstd_vals = lax.rsqrt(jnp.mean(centered * centered, axis=-1, keepdims=True) + EPS)
    return centered * rstd_vals, rstd_vals


def temporal_kernel(info_ref, count_ref, *refs):
    n = 4
    piece_refs = refs[: 2 * n]
    w_ref, cot_own_ref, cot_other_ref = refs[2 * n : 2 * n + 3]
    (tout_own_ref, tout_other_ref, hid_ref, gp_ref, gh_own_ref, gh_other_ref) = refs[
        2 * n + 3 : 2 * n + 9
    ]
    pj_ref, prod_ref, score_ref, weight_ref, wide_ref = refs[2 * n + 9 :]
    rows = TILE
    for i in range(2 * n):
        hid_ref[i * rows : (i + 1) * rows, :] = normalize(piece_refs[i][...])[0].astype(BF16)
    pj_ref[...] = dot_nn(hid_ref[...], w_ref[...]).astype(BF16)
    lane = lax.broadcasted_iota(jnp.int32, (HALF, 128), 0) // HEAD_DIM
    head = lax.broadcasted_iota(jnp.int32, (HALF, 128), 1)
    gather_heads = jnp.where(lane == head, 1.0, 0.0).astype(BF16)
    lane = lax.broadcasted_iota(jnp.int32, (128, HALF), 1) // HEAD_DIM
    head = lax.broadcasted_iota(jnp.int32, (128, HALF), 0)
    spread_heads = jnp.where(lane == head, 1.0, 0.0).astype(BF16)
    frames = [lax.rem(info_ref[0] + n - k, n) for k in range(n)]
    for clip in range(2):
        cot_ref = (cot_own_ref, cot_other_ref)[clip]
        tout_ref = (tout_own_ref, tout_other_ref)[clip]

        def part(k, which):
            at = (clip * n + k) * rows
            return pj_ref[at : at + rows, which * HALF : (which + 1) * HALF]

        queries = [part(k, 0) for k in range(n)]
        keys_in = [part(k, 1) for k in range(n)]
        values_in = [part(k, 2) for k in range(n)]
        cots = [cot_ref[frames[k]] for k in range(n)]
        for f in range(n):
            for g in range(n):
                at = (f * n + g) * rows
                prod_ref[at : at + rows, :] = queries[f] * keys_in[g]
                at += n * n * rows
                prod_ref[at : at + rows, :] = cots[f] * values_in[g]
        score_ref[...] = dot_nn(prod_ref[...], gather_heads)
        valid = [jnp.where(frames[k] < count_ref[clip], 1.0, 0.0) for k in range(n)]
        for f in range(n):
            raised, grad_probs = [], []
            for g in range(n):
                at = (f * n + g) * rows
                raised.append(jnp.exp(score_ref[at : at + rows, :] * SCALE) * valid[g])
                at += n * n * rows
                grad_probs.append(score_ref[at : at + rows, :])
            total = (raised[0] + raised[1]) + (raised[2] + raised[3])
            inverse = 1.0 / total
            probs = [r * inverse for r in raised]
            terms = [a * b for a, b in zip(grad_probs, probs)]
            delta = (terms[0] + terms[1]) + (terms[2] + terms[3])
            for g in range(n):
                at = (f * n + g) * rows
                weight_ref[at : at + rows, :] = probs[g].astype(BF16)
                at += n * n * rows
                weight_ref[at : at + rows, :] = (
                    probs[g] * (grad_probs[g] - delta) * SCALE
                ).astype(BF16)
        wide_ref[...] = dot_nn(weight_ref[...], spread_heads)

        def prob(f, g):
            at = (f * n + g) * rows
            return wide_ref[at : at + rows, :]

        def grad_score(f, g):
            at = (n * n + f * n + g) * rows
            return wide_ref[at : at + rows, :]

        for k in range(n):
            at = (clip * n + k) * rows
            out = sum(prob(k, g) * values_in[g].astype(F32) for g in range(n))
            tout_ref[frames[k]] = out.astype(BF16)
            grad_q = sum(grad_score(k, g) * keys_in[g].astype(F32) for g in range(n))
            grad_k = sum(grad_score(f, k) * queries[f].astype(F32) for f in range(n))
            grad_v = sum(prob(f, k) * cots[f].astype(F32) for f in range(n))
            gp_ref[at : at + rows, 0:HALF] = grad_q.astype(BF16)
            gp_ref[at : at + rows, HALF : 2 * HALF] = grad_k.astype(BF16)
            gp_ref[at : at + rows, 2 * HALF : 3 * HALF] = grad_v.astype(BF16)
    gh_other_ref[...] = dot_nt(gp_ref[n * rows :, :], w_ref[...]).astype(BF16)
    gh_own_ref[...] = dot_nt(gp_ref[: n * rows, :], w_ref[...])


def term_rows(along_x, info_ref, chunk, inner, n):
    if along_x:
        at = lax.rem(info_ref[2] + chunk, n) * (n * CHIP_ROWS) + inner * CHIP_ROWS
    else:
        at = inner * (n * CHIP_ROWS) + lax.rem(info_ref[3] + chunk, n) * CHIP_ROWS
    return pl.ds(pl.multiple_of(at, 8), CHIP_ROWS)


def term_qkv_kernel(info_ref, left_ref, right_ref, *refs):
    n, half = 4, 2
    acc_ref = refs[-1]
    acc_ref[...] = dot_tn(left_ref[...], right_ref[...])
    for side in range(2):
        columns = slice(0, QKV_CUT) if side == 0 else slice(QKV_CUT, 3 * HALF)
        up_ref, down_ref, up_later_ref, down_later_ref, keep_ref = refs[5 * side : 5 * side + 5]

        def block(chunk, inner):
            return acc_ref[term_rows(side == 0, info_ref, chunk, inner, n), columns].astype(BF16)

        for j in range(half):
            up_ref[j] = block(2, j)
            up_ref[half + j] = block(1, half + j)
            down_ref[j] = block(2, half + j)
            down_ref[half + j] = block(3, j)
            up_later_ref[j] = block(1, j)
            down_later_ref[j] = block(3, half + j)
        for j in range(n):
            keep_ref[j] = block(0, j)


def pair_term_kernel(a_own_ref, a_other_ref, g_own_ref, g_other_ref, out_ref):
    total = dot_tn(a_own_ref[...], g_own_ref[...])
    out_ref[...] = (total + dot_tn(a_other_ref[...], g_other_ref[...])).astype(BF16)


def ring_sum_kernel(info_ref, *refs):
    n, half = 4, 2
    inputs, outputs = refs[:10], refs[10:]
    for side in range(2):
        keep, up, down, up_later, down_later = inputs[5 * side : 5 * side + 5]
        place = info_ref[3 - side]
        for j in range(n):
            if j < half:
                terms = (keep[j], down[half + j], up_later[j])
            else:
                terms = (keep[j], up[j], down_later[j - half])
            total = terms[0].astype(F32) + terms[1].astype(F32) + terms[2].astype(F32)
            total = total.astype(BF16)
            for k in range(n):

                @pl.when(lax.rem(place + k, n) == j)
                def _(k=k):
                    outputs[4 * side + k][...] = total


def share_kernel(*refs):
    blocks_ref = refs[8]
    total = blocks_ref[0].astype(F32)
    for chip in range(1, blocks_ref.shape[0]):
        total = total + blocks_ref[chip].astype(F32)
    total = total.astype(BF16)
    for side in range(2):
        part = refs[4 * side][...].astype(F32)
        for ref in refs[4 * side + 1 : 4 * side + 4]:
            part = part + ref[...].astype(F32)
        cut = part.shape[1]
        refs[9 + side][:, :cut] = part.astype(BF16)
        refs[9 + side][:, cut:] = total[:, :OUT_CUT] if side == 0 else total[:, OUT_CUT:]


def add_kernel(count, *refs):
    for i in range(len(refs) // (count + 1)):
        total = refs[i * count][...].astype(F32)
        for ref in refs[i * count + 1 : (i + 1) * count]:
            total = total + ref[...].astype(F32)
        out_ref = refs[-(len(refs) // (count + 1)) + i]
        out_ref[...] = total.astype(out_ref.dtype)


def norm_back_kernel(*refs):
    n = 4
    piece_refs = refs[:n]
    own_ref, other_ref = refs[n : n + 2]
    for k in range(n):
        rows = slice(k * TILE, (k + 1) * TILE)
        grad_hidden = own_ref[rows, :] + other_ref[rows, :].astype(F32)
        normed, rstd_vals = normalize(piece_refs[k][...])
        inner = grad_hidden - jnp.mean(grad_hidden, axis=-1, keepdims=True)
        inner = inner - normed * jnp.mean(grad_hidden * normed, axis=-1, keepdims=True)
        refs[n + 2 + k][...] = (rstd_vals * inner).astype(BF16)


def grad_inputs_kernel(info_ref, cot_ref, *refs):
    n = 4
    out_ref, mine_ref, theirs_ref = refs[n:]
    for k in range(n):
        at = pl.multiple_of(lax.rem(info_ref[0] + k, n) * TILE, TILE)
        rows = pl.ds(at, TILE)
        out_ref[rows, :] = (cot_ref[rows, :].astype(F32) + refs[k][...].astype(F32)).astype(BF16)
    first, second = out_ref[:, :HALF], out_ref[:, HALF:]
    is_first = info_ref[1] == 0
    mine_ref[...] = jnp.where(is_first, first, second)
    theirs_ref[...] = jnp.where(is_first, second, first)


def per_device(
    inputs, qkv_spatial, tile_list, tile_count, frame_count, w_out, w_qkv, cot_y, cot_out
):
    seq_count = lax.axis_size("seq")
    fsdp_count = lax.axis_size("fsdp")
    tok_frame = inputs.shape[2]
    place = lax.axis_index("seq")
    core = lax.axis_index("fsdp") % 2
    chip = lax.axis_index("fsdp") // 2
    info = jnp.stack([place, core, chip // 4, chip % 4]).astype(jnp.int32)
    pairs = [(i, i ^ 1) for i in range(fsdp_count)]
    groups = [list(range(c, fsdp_count, 2)) for c in range(2)]
    first_core = core == 0

    def swap(values):
        return lax.ppermute(values, "fsdp", pairs)

    def turn(values, k):
        return lax.ppermute(
            values, "seq", [(i, (i + k) % seq_count) for i in range(seq_count)]
        )

    def along(axis, values, k):
        def moved(i):
            x, z, c = i // 8, i // 2 % 4, i % 2
            x, z = ((x + k) % 4, z) if axis == 0 else (x, (z + k) % 4)
            return x * 8 + z * 2 + c

        return lax.ppermute(values, "fsdp", [(i, moved(i)) for i in range(fsdp_count)])

    def after(values, earlier):
        return lax.optimization_barrier((values, earlier))[0]

    def mirror(values, which):
        return lax.ppermute(
            values, "seq", [(i, i ^ 1 if which == 0 else 3 - i) for i in range(seq_count)]
        )

    def to_chips(blocks):
        return lax.all_to_all(
            blocks, "fsdp", split_axis=0, concat_axis=0, tiled=True, axis_index_groups=groups
        )

    def mine_theirs(first, second):
        return jnp.where(first_core, first, second), jnp.where(first_core, second, first)

    def shaped(shape, dtype=BF16):
        return jax.ShapeDtypeStruct(shape, dtype)

    def half_columns(c):
        cuts = [w_qkv[:, i * D + c * HALF : i * D + (c + 1) * HALF] for i in range(3)]
        return jnp.concatenate(cuts + [w_out[:, c * HALF : (c + 1) * HALF]], axis=1)

    mine, theirs = mine_theirs(half_columns(0), half_columns(1))
    got = swap(theirs)
    top, bottom = mine_theirs(mine, got)
    chip_rows = jnp.concatenate([top, bottom], axis=0)
    chips = fsdp_count // 2
    out_rows = jnp.broadcast_to(chip_rows[None, :, 3 * HALF :], (chips, 2 * w_out.shape[0], HALF))
    half_out = to_chips(out_rows).reshape(D, HALF)
    other_out = swap(half_out)
    qkv_rows = jnp.broadcast_to(
        chip_rows[None, :, : 3 * HALF], (chips, 2 * w_qkv.shape[0], 3 * HALF)
    )
    half_qkv = to_chips(after(qkv_rows, half_out)).reshape(D, 3 * HALF)

    cot_mine, cot_theirs = mine_theirs(cot_out[0][..., :HALF], cot_out[0][..., HALF:])
    cot_other = swap(cot_theirs)
    counts2 = jnp.concatenate([frame_count, swap(frame_count)])

    qkv = qkv_spatial.reshape(tok_frame, 3 * D)
    lists = tile_list.reshape(-1, LIST_LEN)
    counts = tile_count.reshape(-1)
    mask_scratch = pltpu.VMEM((tok_frame, tok_frame), F32)
    attn = call(
        spatial_forward_kernel,
        shaped((tok_frame, D)),
        (lists, counts, qkv),
        [SMEM, SMEM, VMEM],
        [mask_scratch],
        flops=4 * 10**9,
        nbytes=3 * 10**6,
    )
    attn_other = swap(attn)
    resid, full_out, *pieces = call(
        resid_kernel,
        [shaped((tok_frame, D)), shaped((D, D))] + [shaped((TILE, D))] * seq_count,
        (info, inputs.reshape(tok_frame, D), attn, half_out, other_out),
        [SMEM, VMEM, VMEM, VMEM, VMEM],
        flops=2 * 10**9,
        nbytes=4 * 10**6,
    )
    own = [pieces[0]] + [turn(pieces[k], k) for k in range(1, seq_count)]
    other = [swap(piece) for piece in own]
    wide = 2 * seq_count * seq_count * TILE
    rows = seq_count * TILE
    tout_own, tout_other, hidden, grad_proj, gh_own, gh_other = call(
        temporal_kernel,
        [
            shaped((seq_count, TILE, HALF)),
            shaped((seq_count, TILE, HALF)),
            shaped((2 * rows, D)),
            shaped((2 * rows, 3 * HALF)),
            shaped((rows, D), F32),
            shaped((rows, D)),
        ],
        (info, counts2, *own, *other, half_qkv, cot_mine, cot_other),
        [SMEM, SMEM] + [VMEM] * (2 * seq_count + 3),
        [
            pltpu.VMEM((2 * rows, 3 * HALF), BF16),
            pltpu.VMEM((wide, HALF), BF16),
            pltpu.VMEM((wide, 128), F32),
            pltpu.VMEM((wide, 128), BF16),
            pltpu.VMEM((wide, HALF), F32),
        ],
        flops=10**10,
        nbytes=10**7,
    )
    gh_got = swap(gh_other)
    tout_got = swap(tout_other)
    blocks = []
    for columns in (QKV_CUT, 3 * HALF - QKV_CUT):
        blocks += [shaped((size, CHIP_ROWS, columns)) for size in (4, 4, 2, 2, 4)]
    terms = call(
        term_qkv_kernel,
        blocks,
        (info, hidden, grad_proj),
        [SMEM, VMEM, VMEM],
        [pltpu.VMEM((D, 3 * HALF), F32)],
        flops=2 * 10**9,
        nbytes=7 * 10**6,
    )
    backs = call(
        norm_back_kernel,
        [shaped((TILE, D))] * seq_count,
        (*own, gh_own, gh_got),
        [VMEM] * (seq_count + 2),
        flops=10**8,
        nbytes=3 * 10**6,
    )
    terms = after(terms, backs)
    backs = [backs[0]] + [turn(backs[k], -k) for k in range(1, seq_count)]
    sums = []
    for side in range(2):
        up, down, up_later, down_later, keep = terms[5 * side : 5 * side + 5]
        up, down = along(side, up, 1), along(side, down, -1)
        sums.append([keep, up, down, up_later, down_later])
    sums = after(sums, backs)
    for side in range(2):
        keep, up, down, up_later, down_later = sums[side]
        up_later = (up_later.astype(F32) + up[:2].astype(F32)).astype(BF16)
        down_later = (down_later.astype(F32) + down[:2].astype(F32)).astype(BF16)
        sums[side][3:] = [along(side, up_later, 1), along(side, down_later, -1)]
    grad_x, gx_mine, gx_theirs = call(
        grad_inputs_kernel,
        [shaped((tok_frame, D)), shaped((tok_frame, HALF)), shaped((tok_frame, HALF))],
        (info, cot_y.reshape(tok_frame, D), *backs),
        [SMEM] + [VMEM] * (seq_count + 1),
        flops=10**7,
        nbytes=3 * 10**6,
    )
    gx_got = swap(gx_theirs)
    term_out = call(
        pair_term_kernel,
        shaped((D, HALF)),
        (attn, attn_other, gx_mine, gx_got),
        [VMEM] * 4,
        flops=10**9,
        nbytes=3 * 10**6,
    )
    grad_qkv = call(
        spatial_back_kernel,
        shaped((tok_frame, 3 * D)),
        (lists, counts, qkv, after(grad_x, term_out), full_out),
        [SMEM, SMEM] + [VMEM] * 3,
        [mask_scratch, pltpu.VMEM((tok_frame, D), BF16)],
        flops=10**10,
        nbytes=7 * 10**6,
    )

    out_blocks = to_chips(term_out.reshape(chips, CHIP_ROWS, HALF))
    parts = call(
        ring_sum_kernel,
        [shaped((CHIP_ROWS, QKV_CUT))] * 4 + [shaped((CHIP_ROWS, 3 * HALF - QKV_CUT))] * 4,
        (info, *sums[0], *sums[1]),
        [SMEM] + [VMEM] * 10,
        flops=10**7,
        nbytes=10**7,
    )
    adds = []
    for side in range(2):
        adds += [parts[4 * side]]
        adds += [along(1 - side, parts[4 * side + k], k) for k in (1, 2, 3)]
    chip_share = shaped((CHIP_ROWS, D))
    share = call(
        share_kernel,
        [chip_share] * 2,
        after([*adds, out_blocks], grad_qkv),
        [VMEM] * 9,
        nbytes=3 * 10**6,
    )
    for step in range(2):
        adds = []
        for side in range(2):
            adds += [share[side], mirror(share[side], step ^ side)]
        share = call(
            functools.partial(add_kernel, 2), [chip_share] * 2, adds, [VMEM] * 4, nbytes=10**6
        )
    share = jnp.concatenate(
        [
            share[0][:, :QKV_CUT],
            share[1][:, : 3 * HALF - QKV_CUT],
            share[0][:, QKV_CUT:],
            share[1][:, 3 * HALF - QKV_CUT :],
        ],
        axis=1,
    )
    per = share.shape[0] // 2
    keep, send = mine_theirs(share[:per], share[per:])
    left, right = mine_theirs(keep, swap(send))
    factor = 1.0 / math.sqrt(fsdp_count * seq_count * tok_frame)
    left, right = left.astype(F32) * factor, right.astype(F32) * factor
    grad_w_qkv = jnp.concatenate(
        [side[:, i * HALF : (i + 1) * HALF] for i in range(3) for side in (left, right)], axis=1
    )
    grad_w_out = jnp.concatenate([left[:, 3 * HALF :], right[:, 3 * HALF :]], axis=1)
    tout = jnp.concatenate(mine_theirs(tout_own, tout_got), axis=-1)
    return (
        resid.reshape(inputs.shape),
        tout[None],
        grad_x.reshape(inputs.shape),
        grad_qkv.reshape(qkv_spatial.shape),
        grad_w_out,
        grad_w_qkv,
    )


def solution(mesh):
    placed = (
        P("fsdp", "seq", None, None),
        P("fsdp", "seq", None, None),
        P("fsdp", "seq", None, None),
        P("fsdp", "seq", None),
        P("fsdp"),
        P("fsdp", None),
        P("fsdp", None),
        P("fsdp", "seq", None, None),
        P("fsdp", None, "seq", None),
    )
    return jax.shard_map(
        per_device,
        mesh=mesh,
        in_specs=placed,
        out_specs=(
            P("fsdp", "seq", None, None),
            P("fsdp", None, "seq", None),
            P("fsdp", "seq", None, None),
            P("fsdp", "seq", None, None),
            P("fsdp", None),
            P("fsdp", None),
        ),
        check_vma=False,
    )
```

```python
import functools
import math

import jax
import jax.numpy as jnp
from jax import lax
from jax.experimental import pallas as pl
from jax.experimental.pallas import tpu as pltpu
from jax.sharding import PartitionSpec as P

D = 1152
HEADS = 16
HEAD_DIM = 72
TILE = 64
LIST_LEN = 3
HALF = D // 2
CHIP_ROWS = 72
EPS = 1e-06
SCALE = HEAD_DIM ** (-0.5)
F32 = jnp.float32
BF16 = jnp.bfloat16
VMEM = pl.BlockSpec(memory_space=pltpu.VMEM)
SMEM = pl.BlockSpec(memory_space=pltpu.SMEM)


def dot_nn(a, b):
    return lax.dot_general(a, b, (((1,), (0,)), ((), ())), preferred_element_type=F32)


def dot_nt(a, b):
    return lax.dot_general(a, b, (((1,), (1,)), ((), ())), preferred_element_type=F32)


def dot_tn(a, b):
    return lax.dot_general(a, b, (((0,), (0,)), ((), ())), preferred_element_type=F32)


def call(kernel, out_shape, operands, specs, scratch=(), limit=12, flops=0, nbytes=0):
    many = isinstance(out_shape, (list, tuple))
    return pl.pallas_call(
        kernel,
        out_shape=out_shape,
        in_specs=specs,
        out_specs=[VMEM] * len(out_shape) if many else VMEM,
        scratch_shapes=list(scratch),
        compiler_params=pltpu.CompilerParams(vmem_limit_bytes=limit << 20),
        cost_estimate=pl.CostEstimate(flops=flops, bytes_accessed=nbytes, transcendentals=0),
    )(*operands)


def head_window(head):
    low = head * HEAD_DIM
    start = low // 128 * 128
    stop = -(-(low + HEAD_DIM) // 128) * 128
    lane = lax.broadcasted_iota(jnp.int32, (1, stop - start), 1) + start
    inside = (lane >= low) & (lane < low + HEAD_DIM)
    return start, stop, inside


def key_mask(list_ref, count_ref, mask_ref):
    rows = mask_ref.shape[0]
    key_tile = lax.broadcasted_iota(jnp.int32, (TILE, rows), 1) // TILE
    for j in range(rows // TILE):
        live = jnp.zeros((TILE, rows), F32)
        for m in range(LIST_LEN):
            named = jnp.where(m < count_ref[j], list_ref[j, m], -1)
            live = jnp.where(key_tile == named, 1.0, live)
        mask_ref[j * TILE : (j + 1) * TILE, :] = live


def head_probs(qkv_ref, mask, start, stop, inside):
    queries = qkv_ref[:, start:stop]
    keys_in = jnp.where(inside, qkv_ref[:, D + start : D + stop], 0.0).astype(BF16)
    values_in = jnp.where(inside, qkv_ref[:, 2 * D + start : 2 * D + stop], 0.0).astype(BF16)
    raised = jnp.exp(dot_nt(queries, keys_in) * SCALE) * mask
    probs = raised * (1.0 / jnp.sum(raised, axis=-1, keepdims=True))
    return queries, keys_in, values_in, probs


def spatial_forward_kernel(list_ref, count_ref, qkv_ref, attn_ref, mask_ref):
    key_mask(list_ref, count_ref, mask_ref)
    attn_ref[...] = jnp.zeros_like(attn_ref)
    for head in range(HEADS):
        start, stop, inside = head_window(head)
        _, _, values_in, probs = head_probs(qkv_ref, mask_ref[...], start, stop, inside)
        mixed = dot_nn(probs.astype(BF16), values_in).astype(BF16)
        attn_ref[:, start:stop] = attn_ref[:, start:stop] + mixed


def spatial_back_kernel(
    info_ref,
    list_ref,
    count_ref,
    qkv_ref,
    gx_ref,
    w_ref,
    tout_own_ref,
    tout_got_ref,
    out_ref,
    tout_ref,
    mask_ref,
    ga_ref,
):
    is_first = info_ref[1] == 0
    for k in range(tout_ref.shape[0]):
        own, got = tout_own_ref[k], tout_got_ref[k]
        tout_ref[k, :, :HALF] = jnp.where(is_first, own, got)
        tout_ref[k, :, HALF:] = jnp.where(is_first, got, own)
    key_mask(list_ref, count_ref, mask_ref)
    ga_ref[...] = dot_nt(gx_ref[...], w_ref[...]).astype(BF16)
    out_ref[...] = jnp.zeros_like(out_ref)
    for head in range(HEADS):
        start, stop, inside = head_window(head)
        queries, keys_in, values_in, probs = head_probs(
            qkv_ref, mask_ref[...], start, stop, inside
        )
        grad = jnp.where(inside, ga_ref[:, start:stop], 0.0).astype(BF16)
        queries = jnp.where(inside, queries, 0.0).astype(BF16)
        grad_probs = dot_nt(grad, values_in)
        delta = jnp.sum(grad_probs * probs, axis=-1, keepdims=True)
        grad_scores = (probs * (grad_probs - delta) * SCALE).astype(BF16)
        for offset, part in (
            (0, dot_nn(grad_scores, keys_in)),
            (D, dot_tn(grad_scores, queries)),
            (2 * D, dot_tn(probs.astype(BF16), grad)),
        ):
            where = (slice(None), slice(offset + start, offset + stop))
            out_ref[where] = out_ref[where] + part.astype(BF16)


def resid_kernel(info_ref, x_ref, attn_ref, own_ref, other_ref, resid_ref, w_ref):
    own, other = own_ref[...], other_ref[...]
    is_first = info_ref[1] == 0
    w_ref[:, :HALF] = jnp.where(is_first, own, other)
    w_ref[:, HALF:] = jnp.where(is_first, other, own)
    resid_ref[...] = (x_ref[...].astype(F32) + dot_nn(attn_ref[...], w_ref[...])).astype(BF16)


def normalize(rows):
    values = rows.astype(F32)
    centered = values - jnp.mean(values, axis=-1, keepdims=True)
    rstd_vals = lax.rsqrt(jnp.mean(centered * centered, axis=-1, keepdims=True) + EPS)
    return centered * rstd_vals, rstd_vals


def term_rows(along_x, info_ref, chunk, inner, n):
    if along_x:
        at = lax.rem(info_ref[2] + chunk, n) * (n * CHIP_ROWS) + inner * CHIP_ROWS
    else:
        at = inner * (n * CHIP_ROWS) + lax.rem(info_ref[3] + chunk, n) * CHIP_ROWS
    return pl.ds(pl.multiple_of(at, 8), CHIP_ROWS)


def write_terms(along_x, info_ref, acc_ref, refs):
    n, half = 4, 2
    up_ref, down_ref, up_later_ref, down_later_ref, keep_ref = refs

    def block(chunk, inner):
        return acc_ref[term_rows(along_x, info_ref, chunk, inner, n), :].astype(BF16)

    for j in range(half):
        up_ref[j] = block(2, j)
        up_ref[half + j] = block(1, half + j)
        down_ref[j] = block(2, half + j)
        down_ref[half + j] = block(3, j)
        up_later_ref[j] = block(1, j)
        down_later_ref[j] = block(3, half + j)
    for j in range(n):
        keep_ref[j] = block(0, j)


def temporal_kernel(
    info_ref,
    count_ref,
    own_ref,
    other_ref,
    w_ref,
    cot_own_ref,
    cot_other_ref,
    tout_own_ref,
    tout_other_ref,
    gh_own_ref,
    gh_other_ref,
    v_term_ref,
    *refs,
):
    term_refs = refs[:5]
    hid_ref, gp_ref, acc_ref, pj_ref, prod_ref, score_ref, weight_ref, wide_ref = refs[5:]
    n = own_ref.shape[0]
    rows = TILE
    for clip, ref in enumerate((own_ref, other_ref)):
        for k in range(n):
            at = (clip * n + k) * rows
            hid_ref[at : at + rows, :] = normalize(ref[k])[0].astype(BF16)
    pj_ref[...] = dot_nn(hid_ref[...], w_ref[...]).astype(BF16)
    lane = lax.broadcasted_iota(jnp.int32, (HALF, 128), 0) // HEAD_DIM
    head = lax.broadcasted_iota(jnp.int32, (HALF, 128), 1)
    gather_heads = jnp.where(lane == head, 1.0, 0.0).astype(BF16)
    lane = lax.broadcasted_iota(jnp.int32, (128, HALF), 1) // HEAD_DIM
    head = lax.broadcasted_iota(jnp.int32, (128, HALF), 0)
    spread_heads = jnp.where(lane == head, 1.0, 0.0).astype(BF16)
    for clip in range(2):
        cot_ref = (cot_own_ref, cot_other_ref)[clip]
        tout_ref = (tout_own_ref, tout_other_ref)[clip]

        def part(k, which):
            at = (clip * n + k) * rows
            return pj_ref[at : at + rows, which * HALF : (which + 1) * HALF]

        queries = [part(k, 0) for k in range(n)]
        keys_in = [part(k, 1) for k in range(n)]
        values_in = [part(k, 2) for k in range(n)]
        cots = [cot_ref[k] for k in range(n)]
        for f in range(n):
            for g in range(n):
                at = (f * n + g) * rows
                prod_ref[at : at + rows, :] = queries[f] * keys_in[g]
                at += n * n * rows
                prod_ref[at : at + rows, :] = cots[f] * values_in[g]
        score_ref[...] = dot_nn(prod_ref[...], gather_heads)
        valid = [jnp.where(k < count_ref[clip], 1.0, 0.0) for k in range(n)]
        for f in range(n):
            raised, grad_probs = [], []
            for g in range(n):
                at = (f * n + g) * rows
                raised.append(jnp.exp(score_ref[at : at + rows, :] * SCALE) * valid[g])
                at += n * n * rows
                grad_probs.append(score_ref[at : at + rows, :])
            total = (raised[0] + raised[1]) + (raised[2] + raised[3])
            inverse = 1.0 / total
            probs = [r * inverse for r in raised]
            terms = [a * b for a, b in zip(grad_probs, probs)]
            delta = (terms[0] + terms[1]) + (terms[2] + terms[3])
            for g in range(n):
                at = (f * n + g) * rows
                weight_ref[at : at + rows, :] = probs[g].astype(BF16)
                at += n * n * rows
                weight_ref[at : at + rows, :] = (
                    probs[g] * (grad_probs[g] - delta) * SCALE
                ).astype(BF16)
        wide_ref[...] = dot_nn(weight_ref[...], spread_heads)

        def prob(f, g):
            at = (f * n + g) * rows
            return wide_ref[at : at + rows, :]

        def grad_score(f, g):
            at = (n * n + f * n + g) * rows
            return wide_ref[at : at + rows, :]

        for k in range(n):
            at = (clip * n + k) * rows
            out = sum(prob(k, g) * values_in[g].astype(F32) for g in range(n))
            tout_ref[k] = out.astype(BF16)
            grad_q = sum(grad_score(k, g) * keys_in[g].astype(F32) for g in range(n))
            grad_k = sum(grad_score(f, k) * queries[f].astype(F32) for f in range(n))
            grad_v = sum(prob(f, k) * cots[f].astype(F32) for f in range(n))
            gp_ref[at : at + rows, 0:HALF] = grad_q.astype(BF16)
            gp_ref[at : at + rows, HALF : 2 * HALF] = grad_k.astype(BF16)
            gp_ref[at : at + rows, 2 * HALF : 3 * HALF] = grad_v.astype(BF16)
    gh_other_ref[...] = dot_nt(gp_ref[n * rows :, :], w_ref[...]).astype(BF16)
    gh_own_ref[...] = dot_nt(gp_ref[: n * rows, :], w_ref[...])
    acc_ref[...] = dot_tn(hid_ref[...], gp_ref[:, : 2 * HALF])
    write_terms(True, info_ref, acc_ref, term_refs)
    v_term_ref[...] = dot_tn(hid_ref[...], gp_ref[:, 2 * HALF :])


def second_term_kernel(
    info_ref, v_ref, attn_own_ref, attn_other_ref, gx_own_ref, gx_other_ref, *refs
):
    acc_ref = refs[-1]
    acc_ref[:, :HALF] = v_ref[...]
    total = jnp.zeros((D, HALF), F32)
    for attn_ref, gx_ref in ((attn_own_ref, gx_own_ref), (attn_other_ref, gx_other_ref)):
        total = total + dot_tn(attn_ref[...], gx_ref[...])
    acc_ref[:, HALF:] = total
    write_terms(False, info_ref, acc_ref, refs[:-1])


def ring_sum_kernel(info_ref, *refs):
    n, half = 4, 2
    inputs, outputs = refs[:10], refs[10:]
    for side in range(2):
        keep, up, down, up_later, down_later = inputs[5 * side : 5 * side + 5]
        place = info_ref[3 - side]
        for j in range(n):
            if j < half:
                terms = (keep[j], down[half + j], up_later[j])
            else:
                terms = (keep[j], up[j], down_later[j - half])
            total = terms[0].astype(F32) + terms[1].astype(F32) + terms[2].astype(F32)
            total = total.astype(BF16)
            for k in range(n):

                @pl.when(lax.rem(place + k, n) == j)
                def _(k=k):
                    outputs[4 * side + k][...] = total


def share_kernel(info_ref, *refs):
    keep_ref, send_ref, share_ref = refs[8:]
    for side in range(2):
        part = refs[4 * side][...].astype(F32)
        for ref in refs[4 * side + 1 : 4 * side + 4]:
            part = part + ref[...].astype(F32)
        share_ref[:, side * D : (side + 1) * D] = part
    per = keep_ref.shape[0]
    first, second = share_ref[:per, :], share_ref[per:, :]
    is_first = info_ref[1] == 0
    keep_ref[...] = jnp.where(is_first, first, second).astype(BF16)
    send_ref[...] = jnp.where(is_first, second, first).astype(BF16)


def final_kernel(factor, info_ref, a_ref, a_got_ref, b_ref, b_got_ref, out_ref, qkv_ref):
    mine = (a_ref[...].astype(F32) + a_got_ref[...].astype(F32)) * factor
    partner = (b_ref[...].astype(F32) + b_got_ref[...].astype(F32)) * factor
    is_first = info_ref[1] == 0
    left = jnp.where(is_first, mine, partner)
    right = jnp.where(is_first, partner, mine)
    for i in range(3):
        columns = slice(i * HALF, (i + 1) * HALF)
        qkv_ref[:, i * D : i * D + HALF] = left[:, columns]
        qkv_ref[:, i * D + HALF : (i + 1) * D] = right[:, columns]
    out_ref[:, :HALF] = left[:, 3 * HALF :]
    out_ref[:, HALF:] = right[:, 3 * HALF :]


def add_kernel(count, *refs):
    for i in range(len(refs) // (count + 1)):
        total = refs[i * count][...].astype(F32)
        for ref in refs[i * count + 1 : (i + 1) * count]:
            total = total + ref[...].astype(F32)
        out_ref = refs[-(len(refs) // (count + 1)) + i]
        out_ref[...] = total.astype(out_ref.dtype)


def norm_back_kernel(
    info_ref, resid_ref, own_ref, other_ref, pair_ref, out_ref, mine_ref, theirs_ref
):
    is_first = info_ref[1] == 0
    for k in range(resid_ref.shape[0]):
        rows = slice(k * TILE, (k + 1) * TILE)
        grad_hidden = own_ref[rows, :] + other_ref[rows, :].astype(F32)
        normed, rstd_vals = normalize(resid_ref[k])
        inner = grad_hidden - jnp.mean(grad_hidden, axis=-1, keepdims=True)
        inner = inner - normed * jnp.mean(grad_hidden * normed, axis=-1, keepdims=True)
        norm_back = (rstd_vals * inner).astype(BF16).astype(F32)
        out_ref[k] = (pair_ref[k, :, :D].astype(F32) + norm_back).astype(BF16)
        first, second = out_ref[k, :, :HALF], out_ref[k, :, HALF:]
        mine_ref[rows, :] = jnp.where(is_first, first, second)
        theirs_ref[rows, :] = jnp.where(is_first, second, first)


def per_device(
    inputs, qkv_spatial, tile_list, tile_count, frame_count, w_out, w_qkv, cot_y, cot_out
):
    seq_count = lax.axis_size("seq")
    fsdp_count = lax.axis_size("fsdp")
    tok_frame = inputs.shape[2]
    place = lax.axis_index("seq")
    core = lax.axis_index("fsdp") % 2
    chip = lax.axis_index("fsdp") // 2
    info = jnp.stack([place, core, chip // 4, chip % 4]).astype(jnp.int32)
    pairs = [(i, i ^ 1) for i in range(fsdp_count)]
    groups = [list(range(c, fsdp_count, 2)) for c in range(2)]
    first_core = core == 0

    def swap(values):
        return lax.ppermute(values, "fsdp", pairs)

    def over_seq(blocks):
        return lax.all_to_all(blocks, "seq", split_axis=0, concat_axis=0, tiled=True)

    def along(axis, values, k):
        def moved(i):
            x, z, c = i // 8, i // 2 % 4, i % 2
            x, z = ((x + k) % 4, z) if axis == 0 else (x, (z + k) % 4)
            return x * 8 + z * 2 + c

        return lax.ppermute(values, "fsdp", [(i, moved(i)) for i in range(fsdp_count)])

    def after(values, earlier):
        return lax.optimization_barrier((values, earlier))[0]

    def mirror(values, which):
        return lax.ppermute(
            values, "seq", [(i, i ^ 1 if which == 0 else 3 - i) for i in range(seq_count)]
        )

    def to_chips(blocks):
        return lax.all_to_all(
            blocks, "fsdp", split_axis=0, concat_axis=0, tiled=True, axis_index_groups=groups
        )

    def mine_theirs(first, second):
        return jnp.where(first_core, first, second), jnp.where(first_core, second, first)

    def shaped(shape, dtype=BF16):
        return jax.ShapeDtypeStruct(shape, dtype)

    def half_columns(c):
        cuts = [w_qkv[:, i * D + c * HALF : i * D + (c + 1) * HALF] for i in range(3)]
        return jnp.concatenate(cuts + [w_out[:, c * HALF : (c + 1) * HALF]], axis=1)

    mine, theirs = mine_theirs(half_columns(0), half_columns(1))
    got = swap(theirs)
    top, bottom = mine_theirs(mine, got)
    chip_rows = jnp.concatenate([top, bottom], axis=0)
    half_qkv = lax.all_gather(
        chip_rows[:, : 3 * HALF], "fsdp", axis=0, tiled=True, axis_index_groups=groups
    )
    cot_mine, cot_theirs = mine_theirs(cot_out[0][..., :HALF], cot_out[0][..., HALF:])
    cot_other = swap(cot_theirs)
    counts2 = jnp.concatenate([frame_count, swap(frame_count)])

    qkv = qkv_spatial.reshape(tok_frame, 3 * D)
    lists = tile_list.reshape(-1, LIST_LEN)
    counts = tile_count.reshape(-1)
    mask_scratch = pltpu.VMEM((tok_frame, tok_frame), F32)
    attn = call(
        spatial_forward_kernel,
        shaped((tok_frame, D)),
        (lists, counts, qkv),
        [SMEM, SMEM, VMEM],
        [mask_scratch],
        flops=4 * 10**9,
        nbytes=3 * 10**6,
    )
    chips = fsdp_count // 2
    out_rows = jnp.broadcast_to(chip_rows[None, :, 3 * HALF :], (chips, 2 * w_out.shape[0], HALF))
    half_out = to_chips(after(out_rows, (attn, cot_mine, cot_theirs))).reshape(D, HALF)
    other_out = swap(half_out)
    resid, full_out = call(
        resid_kernel,
        [shaped((tok_frame, D)), shaped((D, D))],
        (info, inputs.reshape(tok_frame, D), attn, half_out, other_out),
        [SMEM, VMEM, VMEM, VMEM, VMEM],
        limit=16,
        flops=2 * 10**9,
        nbytes=4 * 10**6,
    )
    own = over_seq(resid.reshape(seq_count, TILE, D))
    other = swap(own)
    pair = jnp.concatenate([cot_y.reshape(tok_frame, D), attn], axis=1)
    pair = over_seq(after(pair, own).reshape(seq_count, TILE, 2 * D))
    attn_own = pair[..., D:].reshape(tok_frame, D)
    attn_other = swap(attn_own)
    wide = 2 * seq_count * seq_count * TILE
    rows = seq_count * TILE
    blocks = [shaped((size, CHIP_ROWS, D)) for size in (4, 4, 2, 2, 4)]
    tout_own, tout_other, gh_own, gh_other, v_term, *first_terms = call(
        temporal_kernel,
        [
            shaped((seq_count, TILE, HALF)),
            shaped((seq_count, TILE, HALF)),
            shaped((rows, D), F32),
            shaped((rows, D)),
            shaped((D, HALF), F32),
        ]
        + blocks,
        (info, counts2, own, other, half_qkv, cot_mine, cot_other),
        [SMEM, SMEM] + [VMEM] * 5,
        [
            pltpu.VMEM((2 * rows, D), BF16),
            pltpu.VMEM((2 * rows, 3 * HALF), BF16),
            pltpu.VMEM((D, D), F32),
            pltpu.VMEM((2 * rows, 3 * HALF), BF16),
            pltpu.VMEM((wide, HALF), BF16),
            pltpu.VMEM((wide, 128), F32),
            pltpu.VMEM((wide, 128), BF16),
            pltpu.VMEM((wide, HALF), F32),
        ],
        limit=58,
        flops=10**10,
        nbytes=10**7,
    )
    gh_got = swap(gh_other)
    grad_x, gx_mine, gx_theirs = call(
        norm_back_kernel,
        [shaped((seq_count, TILE, D))] + [shaped((rows, HALF))] * 2,
        (info, own, gh_own, gh_got, pair),
        [SMEM] + [VMEM] * 4,
        flops=10**8,
        nbytes=3 * 10**6,
    )
    gx_got = swap(gx_theirs)
    second_terms = call(
        second_term_kernel,
        blocks,
        (info, v_term, attn_own, attn_other, gx_mine, gx_got),
        [SMEM] + [VMEM] * 5,
        [pltpu.VMEM((D, D), F32)],
        limit=24,
        flops=2 * 10**9,
        nbytes=5 * 10**6,
    )
    grad_x = over_seq(after(grad_x, second_terms)).reshape(tok_frame, D)
    first_terms = after(first_terms, second_terms)
    sums = []
    for side, terms in enumerate((first_terms, second_terms)):
        up, down, up_later, down_later, keep = terms
        up, down = along(side, up, 1), along(side, down, -1)
        up_later = (up_later.astype(F32) + up[:2].astype(F32)).astype(BF16)
        down_later = (down_later.astype(F32) + down[:2].astype(F32)).astype(BF16)
        sums.append([keep, up, down, up_later, down_later])
    tout_got = swap(after(tout_other, sums))
    grad_qkv, tout = call(
        spatial_back_kernel,
        [shaped((tok_frame, 3 * D)), shaped((seq_count, TILE, D))],
        (info, lists, counts, qkv, after(grad_x, sums), full_out, tout_own, tout_got),
        [SMEM] * 3 + [VMEM] * 5,
        [mask_scratch, pltpu.VMEM((tok_frame, D), BF16)],
        limit=56,
        flops=10**10,
        nbytes=7 * 10**6,
    )
    for side in range(2):
        sums[side][3:] = [along(side, sums[side][3], 1), along(side, sums[side][4], -1)]
    chip_share = shaped((CHIP_ROWS, D))
    parts = call(
        ring_sum_kernel,
        [chip_share] * 8,
        after((info, *sums[0], *sums[1]), grad_qkv),
        [SMEM] + [VMEM] * 10,
        flops=10**7,
        nbytes=10**7,
    )
    adds = []
    for side in range(2):
        adds += [parts[4 * side]]
        adds += [along(1 - side, parts[4 * side + k], k) for k in (1, 2, 3)]
    per = w_out.shape[0]
    keep, send = call(
        share_kernel,
        [shaped((per, 4 * HALF))] * 2,
        (info, *adds),
        [SMEM] + [VMEM] * 8,
        [pltpu.VMEM((CHIP_ROWS, 4 * HALF), F32)],
        nbytes=3 * 10**6,
    )
    got = swap(send)
    keep, got = call(
        functools.partial(add_kernel, 2),
        [shaped((per, 4 * HALF))] * 2,
        (keep, mirror(keep, 0), got, mirror(got, 1)),
        [VMEM] * 4,
        nbytes=10**6,
    )
    grad_w_out, grad_w_qkv = call(
        functools.partial(final_kernel, 1.0 / math.sqrt(fsdp_count * seq_count * tok_frame)),
        [shaped((per, D), F32), shaped((per, 3 * D), F32)],
        (info, keep, mirror(keep, 1), got, mirror(got, 0)),
        [SMEM] + [VMEM] * 4,
        nbytes=10**6,
    )
    return (
        resid.reshape(inputs.shape),
        tout[None],
        grad_x.reshape(inputs.shape),
        grad_qkv.reshape(qkv_spatial.shape),
        grad_w_out,
        grad_w_qkv,
    )


def solution(mesh):
    placed = (
        P("fsdp", "seq", None, None),
        P("fsdp", "seq", None, None),
        P("fsdp", "seq", None, None),
        P("fsdp", "seq", None),
        P("fsdp"),
        P("fsdp", None),
        P("fsdp", None),
        P("fsdp", "seq", None, None),
        P("fsdp", None, "seq", None),
    )
    return jax.shard_map(
        per_device,
        mesh=mesh,
        in_specs=placed,
        out_specs=(
            P("fsdp", "seq", None, None),
            P("fsdp", None, "seq", None),
            P("fsdp", "seq", None, None),
            P("fsdp", "seq", None, None),
            P("fsdp", None),
            P("fsdp", None),
        ),
        check_vma=False,
    )
```

```python
import functools
import math

import jax
import jax.numpy as jnp
from jax import lax
from jax.experimental import pallas as pl
from jax.experimental.pallas import tpu as pltpu
from jax.sharding import PartitionSpec as P

D = 1152
HEADS = 16
HEAD_DIM = 72
TILE = 64
LIST_LEN = 3
HALF = D // 2
CHIP_ROWS = 72
EPS = 1e-06
SCALE = HEAD_DIM ** (-0.5)
F32 = jnp.float32
BF16 = jnp.bfloat16
VMEM = pl.BlockSpec(memory_space=pltpu.VMEM)
SMEM = pl.BlockSpec(memory_space=pltpu.SMEM)


def dot_nn(a, b):
    return lax.dot_general(a, b, (((1,), (0,)), ((), ())), preferred_element_type=F32)


def dot_nt(a, b):
    return lax.dot_general(a, b, (((1,), (1,)), ((), ())), preferred_element_type=F32)


def dot_tn(a, b):
    return lax.dot_general(a, b, (((0,), (0,)), ((), ())), preferred_element_type=F32)


def call(kernel, out_shape, operands, specs, scratch=(), limit=12, flops=0, nbytes=0):
    many = isinstance(out_shape, (list, tuple))
    return pl.pallas_call(
        kernel,
        out_shape=out_shape,
        in_specs=specs,
        out_specs=[VMEM] * len(out_shape) if many else VMEM,
        scratch_shapes=list(scratch),
        compiler_params=pltpu.CompilerParams(vmem_limit_bytes=limit << 20),
        cost_estimate=pl.CostEstimate(flops=flops, bytes_accessed=nbytes, transcendentals=0),
    )(*operands)


def head_window(head):
    low = head * HEAD_DIM
    start = low // 128 * 128
    stop = -(-(low + HEAD_DIM) // 128) * 128
    lane = lax.broadcasted_iota(jnp.int32, (1, stop - start), 1) + start
    inside = (lane >= low) & (lane < low + HEAD_DIM)
    return start, stop, inside


def key_mask(list_ref, count_ref, mask_ref):
    rows = mask_ref.shape[0]
    key_tile = lax.broadcasted_iota(jnp.int32, (TILE, rows), 1) // TILE
    for j in range(rows // TILE):
        live = jnp.zeros((TILE, rows), F32)
        for m in range(LIST_LEN):
            named = jnp.where(m < count_ref[j], list_ref[j, m], -1)
            live = jnp.where(key_tile == named, 1.0, live)
        mask_ref[j * TILE : (j + 1) * TILE, :] = live


def head_probs(qkv_ref, mask, start, stop, inside):
    queries = qkv_ref[:, start:stop]
    keys_in = jnp.where(inside, qkv_ref[:, D + start : D + stop], 0.0).astype(BF16)
    values_in = jnp.where(inside, qkv_ref[:, 2 * D + start : 2 * D + stop], 0.0).astype(BF16)
    raised = jnp.exp(dot_nt(queries, keys_in) * SCALE) * mask
    probs = raised * (1.0 / jnp.sum(raised, axis=-1, keepdims=True))
    return queries, keys_in, values_in, probs


def spatial_forward_kernel(list_ref, count_ref, qkv_ref, attn_ref, mask_ref):
    key_mask(list_ref, count_ref, mask_ref)
    attn_ref[...] = jnp.zeros_like(attn_ref)
    for head in range(HEADS):
        start, stop, inside = head_window(head)
        _, _, values_in, probs = head_probs(qkv_ref, mask_ref[...], start, stop, inside)
        mixed = dot_nn(probs.astype(BF16), values_in).astype(BF16)
        attn_ref[:, start:stop] = attn_ref[:, start:stop] + mixed


def spatial_back_kernel(
    info_ref,
    list_ref,
    count_ref,
    qkv_ref,
    gx_ref,
    w_ref,
    tout_own_ref,
    tout_got_ref,
    out_ref,
    tout_ref,
    gx_out_ref,
    mask_ref,
    ga_ref,
):
    gx_out_ref[...] = gx_ref[...]
    is_first = info_ref[1] == 0
    for k in range(tout_ref.shape[0]):
        own, got = tout_own_ref[k], tout_got_ref[k]
        tout_ref[k, :, :HALF] = jnp.where(is_first, own, got)
        tout_ref[k, :, HALF:] = jnp.where(is_first, got, own)
    key_mask(list_ref, count_ref, mask_ref)
    ga_ref[...] = dot_nt(gx_ref[...], w_ref[...]).astype(BF16)
    out_ref[...] = jnp.zeros_like(out_ref)
    for head in range(HEADS):
        start, stop, inside = head_window(head)
        queries, keys_in, values_in, probs = head_probs(
            qkv_ref, mask_ref[...], start, stop, inside
        )
        grad = jnp.where(inside, ga_ref[:, start:stop], 0.0).astype(BF16)
        queries = jnp.where(inside, queries, 0.0).astype(BF16)
        grad_probs = dot_nt(grad, values_in)
        delta = jnp.sum(grad_probs * probs, axis=-1, keepdims=True)
        grad_scores = (probs * (grad_probs - delta) * SCALE).astype(BF16)
        for offset, part in (
            (0, dot_nn(grad_scores, keys_in)),
            (D, dot_tn(grad_scores, queries)),
            (2 * D, dot_tn(probs.astype(BF16), grad)),
        ):
            where = (slice(None), slice(offset + start, offset + stop))
            out_ref[where] = out_ref[where] + part.astype(BF16)


def resid_kernel(info_ref, x_ref, attn_ref, own_ref, other_ref, resid_ref, w_ref):
    own, other = own_ref[...], other_ref[...]
    is_first = info_ref[1] == 0
    w_ref[:, :HALF] = jnp.where(is_first, own, other)
    w_ref[:, HALF:] = jnp.where(is_first, other, own)
    resid_ref[...] = (x_ref[...].astype(F32) + dot_nn(attn_ref[...], w_ref[...])).astype(BF16)


def normalize(rows):
    values = rows.astype(F32)
    centered = values - jnp.mean(values, axis=-1, keepdims=True)
    rstd_vals = lax.rsqrt(jnp.mean(centered * centered, axis=-1, keepdims=True) + EPS)
    return centered * rstd_vals, rstd_vals


def term_rows(along_x, info_ref, chunk, inner, n):
    if along_x:
        at = lax.rem(info_ref[2] + chunk, n) * (n * CHIP_ROWS) + inner * CHIP_ROWS
    else:
        at = inner * (n * CHIP_ROWS) + lax.rem(info_ref[3] + chunk, n) * CHIP_ROWS
    return pl.ds(pl.multiple_of(at, 8), CHIP_ROWS)


def write_terms(along_x, info_ref, acc_ref, refs):
    n, half = 4, 2
    up_ref, down_ref, up_later_ref, down_later_ref, keep_ref = refs

    def block(chunk, inner):
        return acc_ref[term_rows(along_x, info_ref, chunk, inner, n), :].astype(BF16)

    for j in range(half):
        up_ref[j] = block(2, j)
        up_ref[half + j] = block(1, half + j)
        down_ref[j] = block(2, half + j)
        down_ref[half + j] = block(3, j)
        up_later_ref[j] = block(1, j)
        down_later_ref[j] = block(3, half + j)
    for j in range(n):
        keep_ref[j] = block(0, j)


def temporal_kernel(
    info_ref,
    own_count_ref,
    other_count_ref,
    own_ref,
    other_ref,
    w_ref,
    cot_own_ref,
    cot_other_ref,
    tout_own_ref,
    tout_other_ref,
    gh_own_ref,
    gh_other_ref,
    v_term_ref,
    *refs,
):
    term_refs = refs[:5]
    hid_ref, gp_ref, acc_ref, pj_ref, prod_ref, score_ref, weight_ref, wide_ref = refs[5:]
    n = own_ref.shape[0]
    rows = TILE
    for clip, ref in enumerate((own_ref, other_ref)):
        for k in range(n):
            at = (clip * n + k) * rows
            hid_ref[at : at + rows, :] = normalize(ref[k])[0].astype(BF16)
    pj_ref[...] = dot_nn(hid_ref[...], w_ref[...]).astype(BF16)
    lane = lax.broadcasted_iota(jnp.int32, (HALF, 128), 0) // HEAD_DIM
    head = lax.broadcasted_iota(jnp.int32, (HALF, 128), 1)
    gather_heads = jnp.where(lane == head, 1.0, 0.0).astype(BF16)
    lane = lax.broadcasted_iota(jnp.int32, (128, HALF), 1) // HEAD_DIM
    head = lax.broadcasted_iota(jnp.int32, (128, HALF), 0)
    spread_heads = jnp.where(lane == head, 1.0, 0.0).astype(BF16)
    for clip in range(2):
        cot_ref = (cot_own_ref, cot_other_ref)[clip]
        tout_ref = (tout_own_ref, tout_other_ref)[clip]

        def part(k, which):
            at = (clip * n + k) * rows
            return pj_ref[at : at + rows, which * HALF : (which + 1) * HALF]

        queries = [part(k, 0) for k in range(n)]
        keys_in = [part(k, 1) for k in range(n)]
        values_in = [part(k, 2) for k in range(n)]
        cots = [cot_ref[k] for k in range(n)]
        for f in range(n):
            for g in range(n):
                at = (f * n + g) * rows
                prod_ref[at : at + rows, :] = queries[f] * keys_in[g]
                at += n * n * rows
                prod_ref[at : at + rows, :] = cots[f] * values_in[g]
        score_ref[...] = dot_nn(prod_ref[...], gather_heads)
        count = (own_count_ref, other_count_ref)[clip][0]
        valid = [jnp.where(k < count, 1.0, 0.0) for k in range(n)]
        for f in range(n):
            raised, grad_probs = [], []
            for g in range(n):
                at = (f * n + g) * rows
                raised.append(jnp.exp(score_ref[at : at + rows, :] * SCALE) * valid[g])
                at += n * n * rows
                grad_probs.append(score_ref[at : at + rows, :])
            total = (raised[0] + raised[1]) + (raised[2] + raised[3])
            inverse = 1.0 / total
            probs = [r * inverse for r in raised]
            terms = [a * b for a, b in zip(grad_probs, probs)]
            delta = (terms[0] + terms[1]) + (terms[2] + terms[3])
            for g in range(n):
                at = (f * n + g) * rows
                weight_ref[at : at + rows, :] = probs[g].astype(BF16)
                at += n * n * rows
                weight_ref[at : at + rows, :] = (
                    probs[g] * (grad_probs[g] - delta) * SCALE
                ).astype(BF16)
        wide_ref[...] = dot_nn(weight_ref[...], spread_heads)

        def prob(f, g):
            at = (f * n + g) * rows
            return wide_ref[at : at + rows, :]

        def grad_score(f, g):
            at = (n * n + f * n + g) * rows
            return wide_ref[at : at + rows, :]

        for k in range(n):
            at = (clip * n + k) * rows
            out = sum(prob(k, g) * values_in[g].astype(F32) for g in range(n))
            tout_ref[k] = out.astype(BF16)
            grad_q = sum(grad_score(k, g) * keys_in[g].astype(F32) for g in range(n))
            grad_k = sum(grad_score(f, k) * queries[f].astype(F32) for f in range(n))
            grad_v = sum(prob(f, k) * cots[f].astype(F32) for f in range(n))
            gp_ref[at : at + rows, 0:HALF] = grad_q.astype(BF16)
            gp_ref[at : at + rows, HALF : 2 * HALF] = grad_k.astype(BF16)
            gp_ref[at : at + rows, 2 * HALF : 3 * HALF] = grad_v.astype(BF16)
    gh_other_ref[...] = dot_nt(gp_ref[n * rows :, :], w_ref[...]).astype(BF16)
    gh_own_ref[...] = dot_nt(gp_ref[: n * rows, :], w_ref[...])
    acc_ref[...] = dot_tn(hid_ref[...], gp_ref[:, : 2 * HALF])
    write_terms(True, info_ref, acc_ref, term_refs)
    v_term_ref[...] = dot_tn(hid_ref[...], gp_ref[:, 2 * HALF :])


def second_term_kernel(
    info_ref, v_ref, attn_own_ref, attn_other_ref, gx_own_ref, gx_other_ref, *refs
):
    acc_ref = refs[-1]
    acc_ref[:, :HALF] = v_ref[...]
    total = jnp.zeros((D, HALF), F32)
    for attn_ref, gx_ref in ((attn_own_ref, gx_own_ref), (attn_other_ref, gx_other_ref)):
        total = total + dot_tn(attn_ref[...], gx_ref[...])
    acc_ref[:, HALF:] = total
    write_terms(False, info_ref, acc_ref, refs[:-1])


def ring_sum_kernel(info_ref, *refs):
    n, half = 4, 2
    inputs, outputs = refs[:10], refs[10:]
    for side in range(2):
        keep, up, down, up_later, down_later = inputs[5 * side : 5 * side + 5]
        place = info_ref[3 - side]
        for j in range(n):
            if j < half:
                terms = (keep[j], down[half + j], up_later[j])
            else:
                terms = (keep[j], up[j], down_later[j - half])
            total = terms[0].astype(F32) + terms[1].astype(F32) + terms[2].astype(F32)
            total = total.astype(BF16)
            for k in range(n):

                @pl.when(lax.rem(place + k, n) == j)
                def _(k=k):
                    outputs[4 * side + k][...] = total


def share_kernel(info_ref, *refs):
    keep_ref, send_ref, share_ref = refs[8:]
    for side in range(2):
        part = refs[4 * side][...].astype(F32)
        for ref in refs[4 * side + 1 : 4 * side + 4]:
            part = part + ref[...].astype(F32)
        share_ref[:, side * D : (side + 1) * D] = part
    per = keep_ref.shape[0]
    first, second = share_ref[:per, :], share_ref[per:, :]
    is_first = info_ref[1] == 0
    keep_ref[...] = jnp.where(is_first, first, second).astype(BF16)
    send_ref[...] = jnp.where(is_first, second, first).astype(BF16)


def final_kernel(factor, info_ref, a_ref, a_got_ref, b_ref, b_got_ref, out_ref, qkv_ref):
    mine = (a_ref[...].astype(F32) + a_got_ref[...].astype(F32)) * factor
    partner = (b_ref[...].astype(F32) + b_got_ref[...].astype(F32)) * factor
    is_first = info_ref[1] == 0
    left = jnp.where(is_first, mine, partner)
    right = jnp.where(is_first, partner, mine)
    for i in range(3):
        columns = slice(i * HALF, (i + 1) * HALF)
        qkv_ref[:, i * D : i * D + HALF] = left[:, columns]
        qkv_ref[:, i * D + HALF : (i + 1) * D] = right[:, columns]
    out_ref[:, :HALF] = left[:, 3 * HALF :]
    out_ref[:, HALF:] = right[:, 3 * HALF :]


def add_kernel(count, *refs):
    for i in range(len(refs) // (count + 1)):
        total = refs[i * count][...].astype(F32)
        for ref in refs[i * count + 1 : (i + 1) * count]:
            total = total + ref[...].astype(F32)
        out_ref = refs[-(len(refs) // (count + 1)) + i]
        out_ref[...] = total.astype(out_ref.dtype)


def norm_back_kernel(
    info_ref, resid_ref, own_ref, other_ref, pair_ref, out_ref, mine_ref, theirs_ref
):
    is_first = info_ref[1] == 0
    for k in range(resid_ref.shape[0]):
        rows = slice(k * TILE, (k + 1) * TILE)
        grad_hidden = own_ref[rows, :] + other_ref[rows, :].astype(F32)
        normed, rstd_vals = normalize(resid_ref[k])
        inner = grad_hidden - jnp.mean(grad_hidden, axis=-1, keepdims=True)
        inner = inner - normed * jnp.mean(grad_hidden * normed, axis=-1, keepdims=True)
        norm_back = (rstd_vals * inner).astype(BF16).astype(F32)
        out_ref[k] = (pair_ref[k, :, :D].astype(F32) + norm_back).astype(BF16)
        first, second = out_ref[k, :, :HALF], out_ref[k, :, HALF:]
        mine_ref[rows, :] = jnp.where(is_first, first, second)
        theirs_ref[rows, :] = jnp.where(is_first, second, first)


def per_device(
    inputs, qkv_spatial, tile_list, tile_count, frame_count, w_out, w_qkv, cot_y, cot_out
):
    seq_count = lax.axis_size("seq")
    fsdp_count = lax.axis_size("fsdp")
    tok_frame = inputs.shape[2]
    place = lax.axis_index("seq")
    core = lax.axis_index("fsdp") % 2
    chip = lax.axis_index("fsdp") // 2
    info = jnp.stack([place, core, chip // 4, chip % 4]).astype(jnp.int32)
    pairs = [(i, i ^ 1) for i in range(fsdp_count)]
    groups = [list(range(c, fsdp_count, 2)) for c in range(2)]
    first_core = core == 0

    def swap(values):
        return lax.ppermute(values, "fsdp", pairs)

    def over_seq(blocks):
        return lax.all_to_all(blocks, "seq", split_axis=0, concat_axis=0, tiled=True)

    def along(axis, values, k):
        def moved(i):
            x, z, c = i // 8, i // 2 % 4, i % 2
            x, z = ((x + k) % 4, z) if axis == 0 else (x, (z + k) % 4)
            return x * 8 + z * 2 + c

        return lax.ppermute(values, "fsdp", [(i, moved(i)) for i in range(fsdp_count)])

    def after(values, earlier):
        return lax.optimization_barrier((values, earlier))[0]

    def mirror(values, which):
        return lax.ppermute(
            values, "seq", [(i, i ^ 1 if which == 0 else 3 - i) for i in range(seq_count)]
        )

    def to_chips(blocks):
        return lax.all_to_all(
            blocks, "fsdp", split_axis=0, concat_axis=0, tiled=True, axis_index_groups=groups
        )

    def mine_theirs(first, second):
        return jnp.where(first_core, first, second), jnp.where(first_core, second, first)

    def shaped(shape, dtype=BF16):
        return jax.ShapeDtypeStruct(shape, dtype)

    def half_columns(c):
        cuts = [w_qkv[:, i * D + c * HALF : i * D + (c + 1) * HALF] for i in range(3)]
        return jnp.concatenate(cuts + [w_out[:, c * HALF : (c + 1) * HALF]], axis=1)

    mine, theirs = mine_theirs(half_columns(0), half_columns(1))
    got = swap(theirs)
    top, bottom = mine_theirs(mine, got)
    chip_rows = jnp.concatenate([top, bottom], axis=0)
    half_qkv = lax.all_gather(
        chip_rows[:, : 3 * HALF], "fsdp", axis=0, tiled=True, axis_index_groups=groups
    )
    cot_mine, cot_theirs = mine_theirs(cot_out[0][..., :HALF], cot_out[0][..., HALF:])
    cot_other = swap(cot_theirs)
    other_count = swap(frame_count)

    qkv = qkv_spatial.reshape(tok_frame, 3 * D)
    lists = tile_list.reshape(-1, LIST_LEN)
    counts = tile_count.reshape(-1)
    mask_scratch = pltpu.VMEM((tok_frame, tok_frame), F32)
    attn = call(
        spatial_forward_kernel,
        shaped((tok_frame, D)),
        (lists, counts, qkv),
        [SMEM, SMEM, VMEM],
        [mask_scratch],
        flops=4 * 10**9,
        nbytes=3 * 10**6,
    )
    chips = fsdp_count // 2
    out_rows = jnp.broadcast_to(chip_rows[None, :, 3 * HALF :], (chips, 2 * w_out.shape[0], HALF))
    half_out = to_chips(after(out_rows, (attn, cot_mine, cot_theirs)))
    other_out = swap(half_out).reshape(D, HALF)
    half_out = half_out.reshape(D, HALF)
    resid, full_out = call(
        resid_kernel,
        [shaped((tok_frame, D)), shaped((D, D))],
        (info, inputs.reshape(tok_frame, D), attn, half_out, other_out),
        [SMEM, VMEM, VMEM, VMEM, VMEM],
        limit=16,
        flops=2 * 10**9,
        nbytes=4 * 10**6,
    )
    own = over_seq(resid.reshape(seq_count, TILE, D))
    other = swap(own)
    pair = jnp.concatenate([cot_y.reshape(tok_frame, D), attn], axis=1)
    pair = over_seq(after(pair, own).reshape(seq_count, TILE, 2 * D))
    attn_own = pair[..., D:].reshape(tok_frame, D)
    attn_other = swap(attn_own)
    wide = 2 * seq_count * seq_count * TILE
    rows = seq_count * TILE
    blocks = [shaped((size, CHIP_ROWS, D)) for size in (4, 4, 2, 2, 4)]
    tout_own, tout_other, gh_own, gh_other, v_term, *first_terms = call(
        temporal_kernel,
        [
            shaped((seq_count, TILE, HALF)),
            shaped((seq_count, TILE, HALF)),
            shaped((rows, D), F32),
            shaped((rows, D)),
            shaped((D, HALF), F32),
        ]
        + blocks,
        (info, frame_count, other_count, own, other, half_qkv, cot_mine, cot_other),
        [SMEM] * 3 + [VMEM] * 5,
        [
            pltpu.VMEM((2 * rows, D), BF16),
            pltpu.VMEM((2 * rows, 3 * HALF), BF16),
            pltpu.VMEM((D, D), F32),
            pltpu.VMEM((2 * rows, 3 * HALF), BF16),
            pltpu.VMEM((wide, HALF), BF16),
            pltpu.VMEM((wide, 128), F32),
            pltpu.VMEM((wide, 128), BF16),
            pltpu.VMEM((wide, HALF), F32),
        ],
        limit=58,
        flops=10**10,
        nbytes=10**7,
    )
    gh_got = swap(gh_other)
    grad_x, gx_mine, gx_theirs = call(
        norm_back_kernel,
        [shaped((seq_count, TILE, D))] + [shaped((rows, HALF))] * 2,
        (info, own, gh_own, gh_got, pair),
        [SMEM] + [VMEM] * 4,
        flops=10**8,
        nbytes=3 * 10**6,
    )
    gx_got = swap(gx_theirs)
    second_terms = call(
        second_term_kernel,
        blocks,
        (info, v_term, attn_own, attn_other, gx_mine, gx_got),
        [SMEM] + [VMEM] * 5,
        [pltpu.VMEM((D, D), F32)],
        limit=24,
        flops=2 * 10**9,
        nbytes=5 * 10**6,
    )
    grad_x = over_seq(after(grad_x, second_terms)).reshape(tok_frame, D)
    first_terms = after(first_terms, second_terms)
    sums = []
    for side, terms in enumerate((first_terms, second_terms)):
        up, down, up_later, down_later, keep = terms
        up, down = along(side, up, 1), along(side, down, -1)
        up_later = (up_later.astype(F32) + up[:2].astype(F32)).astype(BF16)
        down_later = (down_later.astype(F32) + down[:2].astype(F32)).astype(BF16)
        sums.append([keep, up, down, up_later, down_later])
    tout_got = swap(after(tout_other, sums))
    grad_qkv, tout, grad_x = call(
        spatial_back_kernel,
        [shaped((tok_frame, 3 * D)), shaped((seq_count, TILE, D)), shaped((tok_frame, D))],
        (info, lists, counts, qkv, after(grad_x, sums), full_out, tout_own, tout_got),
        [SMEM] * 3 + [VMEM] * 5,
        [mask_scratch, pltpu.VMEM((tok_frame, D), BF16)],
        limit=56,
        flops=10**10,
        nbytes=7 * 10**6,
    )
    for side in range(2):
        sums[side][3:] = [along(side, sums[side][3], 1), along(side, sums[side][4], -1)]
    chip_share = shaped((CHIP_ROWS, D))
    parts = call(
        ring_sum_kernel,
        [chip_share] * 8,
        after((info, *sums[0], *sums[1]), grad_qkv),
        [SMEM] + [VMEM] * 10,
        flops=10**7,
        nbytes=10**7,
    )
    adds = []
    for side in range(2):
        adds += [parts[4 * side]]
        adds += [along(1 - side, parts[4 * side + k], k) for k in (1, 2, 3)]
    per = w_out.shape[0]
    keep, send = call(
        share_kernel,
        [shaped((per, 4 * HALF))] * 2,
        (info, *adds),
        [SMEM] + [VMEM] * 8,
        [pltpu.VMEM((CHIP_ROWS, 4 * HALF), F32)],
        nbytes=3 * 10**6,
    )
    got = swap(send)
    keep, got = call(
        functools.partial(add_kernel, 2),
        [shaped((per, 4 * HALF))] * 2,
        (keep, mirror(keep, 0), got, mirror(got, 1)),
        [VMEM] * 4,
        nbytes=10**6,
    )
    grad_w_out, grad_w_qkv = call(
        functools.partial(final_kernel, 1.0 / math.sqrt(fsdp_count * seq_count * tok_frame)),
        [shaped((per, D), F32), shaped((per, 3 * D), F32)],
        (info, keep, mirror(keep, 1), got, mirror(got, 0)),
        [SMEM] + [VMEM] * 4,
        nbytes=10**6,
    )
    return (
        resid.reshape(inputs.shape),
        tout[None],
        grad_x.reshape(inputs.shape),
        grad_qkv.reshape(qkv_spatial.shape),
        grad_w_out,
        grad_w_qkv,
    )


def solution(mesh):
    placed = (
        P("fsdp", "seq", None, None),
        P("fsdp", "seq", None, None),
        P("fsdp", "seq", None, None),
        P("fsdp", "seq", None),
        P("fsdp"),
        P("fsdp", None),
        P("fsdp", None),
        P("fsdp", "seq", None, None),
        P("fsdp", None, "seq", None),
    )
    return jax.shard_map(
        per_device,
        mesh=mesh,
        in_specs=placed,
        out_specs=(
            P("fsdp", "seq", None, None),
            P("fsdp", None, "seq", None),
            P("fsdp", "seq", None, None),
            P("fsdp", "seq", None, None),
            P("fsdp", None),
            P("fsdp", None),
        ),
        check_vma=False,
    )
```

```python
import functools
import math

import jax
import jax.numpy as jnp
from jax import lax
from jax.experimental import pallas as pl
from jax.experimental.pallas import tpu as pltpu
from jax.sharding import PartitionSpec as P

D = 1152
HEADS = 16
HEAD_DIM = 72
TILE = 64
LIST_LEN = 3
HALF = D // 2
CHIP_ROWS = 72
EPS = 1e-06
SCALE = HEAD_DIM ** (-0.5)
F32 = jnp.float32
BF16 = jnp.bfloat16
VMEM = pl.BlockSpec(memory_space=pltpu.VMEM)
SMEM = pl.BlockSpec(memory_space=pltpu.SMEM)


def dot_nn(a, b):
    return lax.dot_general(a, b, (((1,), (0,)), ((), ())), preferred_element_type=F32)


def dot_nt(a, b):
    return lax.dot_general(a, b, (((1,), (1,)), ((), ())), preferred_element_type=F32)


def dot_tn(a, b):
    return lax.dot_general(a, b, (((0,), (0,)), ((), ())), preferred_element_type=F32)


def call(kernel, out_shape, operands, specs, scratch=(), limit=12, flops=0, nbytes=0):
    many = isinstance(out_shape, (list, tuple))
    return pl.pallas_call(
        kernel,
        out_shape=out_shape,
        in_specs=specs,
        out_specs=[VMEM] * len(out_shape) if many else VMEM,
        scratch_shapes=list(scratch),
        compiler_params=pltpu.CompilerParams(vmem_limit_bytes=limit << 20),
        cost_estimate=pl.CostEstimate(flops=flops, bytes_accessed=nbytes, transcendentals=0),
    )(*operands)


def head_window(head):
    low = head * HEAD_DIM
    start = low // 128 * 128
    stop = -(-(low + HEAD_DIM) // 128) * 128
    lane = lax.broadcasted_iota(jnp.int32, (1, stop - start), 1) + start
    inside = (lane >= low) & (lane < low + HEAD_DIM)
    return start, stop, inside


def key_mask(list_ref, count_ref, mask_ref):
    rows = mask_ref.shape[0]
    key_tile = lax.broadcasted_iota(jnp.int32, (TILE, rows), 1) // TILE
    for j in range(rows // TILE):
        live = jnp.zeros((TILE, rows), F32)
        for m in range(LIST_LEN):
            named = jnp.where(m < count_ref[j], list_ref[j, m], -1)
            live = jnp.where(key_tile == named, 1.0, live)
        mask_ref[j * TILE : (j + 1) * TILE, :] = live


def head_probs(qkv_ref, mask, start, stop, inside):
    queries = qkv_ref[:, start:stop]
    keys_in = jnp.where(inside, qkv_ref[:, D + start : D + stop], 0.0).astype(BF16)
    values_in = jnp.where(inside, qkv_ref[:, 2 * D + start : 2 * D + stop], 0.0).astype(BF16)
    raised = jnp.exp(dot_nt(queries, keys_in) * SCALE) * mask
    probs = raised * (1.0 / jnp.sum(raised, axis=-1, keepdims=True))
    return queries, keys_in, values_in, probs


def spatial_forward_kernel(list_ref, count_ref, qkv_ref, attn_ref, mask_ref):
    key_mask(list_ref, count_ref, mask_ref)
    attn_ref[...] = jnp.zeros_like(attn_ref)
    for head in range(HEADS):
        start, stop, inside = head_window(head)
        _, _, values_in, probs = head_probs(qkv_ref, mask_ref[...], start, stop, inside)
        mixed = dot_nn(probs.astype(BF16), values_in).astype(BF16)
        attn_ref[:, start:stop] = attn_ref[:, start:stop] + mixed


def spatial_back_kernel(
    info_ref,
    list_ref,
    count_ref,
    qkv_ref,
    gx_ref,
    w_own_ref,
    w_other_ref,
    tout_own_ref,
    tout_got_ref,
    out_ref,
    tout_ref,
    gx_out_ref,
    mask_ref,
    ga_ref,
    w_ref,
):
    gx_out_ref[...] = gx_ref[...]
    is_first = info_ref[1] == 0
    for k in range(tout_ref.shape[0]):
        own, got = tout_own_ref[k], tout_got_ref[k]
        tout_ref[k, :, :HALF] = jnp.where(is_first, own, got)
        tout_ref[k, :, HALF:] = jnp.where(is_first, got, own)
    key_mask(list_ref, count_ref, mask_ref)
    own, other = w_own_ref[...], w_other_ref[...]
    w_ref[:, :HALF] = jnp.where(is_first, own, other)
    w_ref[:, HALF:] = jnp.where(is_first, other, own)
    ga_ref[...] = dot_nt(gx_ref[...], w_ref[...]).astype(BF16)
    out_ref[...] = jnp.zeros_like(out_ref)
    for head in range(HEADS):
        start, stop, inside = head_window(head)
        queries, keys_in, values_in, probs = head_probs(
            qkv_ref, mask_ref[...], start, stop, inside
        )
        grad = jnp.where(inside, ga_ref[:, start:stop], 0.0).astype(BF16)
        queries = jnp.where(inside, queries, 0.0).astype(BF16)
        grad_probs = dot_nt(grad, values_in)
        delta = jnp.sum(grad_probs * probs, axis=-1, keepdims=True)
        grad_scores = (probs * (grad_probs - delta) * SCALE).astype(BF16)
        for offset, part in (
            (0, dot_nn(grad_scores, keys_in)),
            (D, dot_tn(grad_scores, queries)),
            (2 * D, dot_tn(probs.astype(BF16), grad)),
        ):
            where = (slice(None), slice(offset + start, offset + stop))
            out_ref[where] = out_ref[where] + part.astype(BF16)


def resid_kernel(info_ref, x_ref, attn_ref, own_ref, other_ref, resid_ref, w_ref):
    own, other = own_ref[...], other_ref[...]
    is_first = info_ref[1] == 0
    w_ref[:, :HALF] = jnp.where(is_first, own, other)
    w_ref[:, HALF:] = jnp.where(is_first, other, own)
    resid_ref[...] = (x_ref[...].astype(F32) + dot_nn(attn_ref[...], w_ref[...])).astype(BF16)


def normalize(rows):
    values = rows.astype(F32)
    centered = values - jnp.mean(values, axis=-1, keepdims=True)
    rstd_vals = lax.rsqrt(jnp.mean(centered * centered, axis=-1, keepdims=True) + EPS)
    return centered * rstd_vals, rstd_vals


def term_rows(along_x, info_ref, chunk, inner, n):
    if along_x:
        at = lax.rem(info_ref[2] + chunk, n) * (n * CHIP_ROWS) + inner * CHIP_ROWS
    else:
        at = inner * (n * CHIP_ROWS) + lax.rem(info_ref[3] + chunk, n) * CHIP_ROWS
    return pl.ds(pl.multiple_of(at, 8), CHIP_ROWS)


def write_terms(along_x, info_ref, acc_ref, refs):
    n, half = 4, 2
    up_ref, down_ref, up_later_ref, down_later_ref, keep_ref = refs

    def block(chunk, inner):
        return acc_ref[term_rows(along_x, info_ref, chunk, inner, n), :].astype(BF16)

    for j in range(half):
        up_ref[j] = block(2, j)
        up_ref[half + j] = block(1, half + j)
        down_ref[j] = block(2, half + j)
        down_ref[half + j] = block(3, j)
        up_later_ref[j] = block(1, j)
        down_later_ref[j] = block(3, half + j)
    for j in range(n):
        keep_ref[j] = block(0, j)


def temporal_kernel(
    info_ref,
    own_count_ref,
    other_count_ref,
    own_ref,
    other_ref,
    w_ref,
    cot_own_ref,
    cot_other_ref,
    tout_own_ref,
    tout_other_ref,
    gh_own_ref,
    gh_other_ref,
    v_term_ref,
    *refs,
):
    term_refs = refs[:5]
    hid_ref, gp_ref, acc_ref, pj_ref, prod_ref, score_ref, weight_ref, wide_ref = refs[5:]
    n = own_ref.shape[0]
    rows = TILE
    for clip, ref in enumerate((own_ref, other_ref)):
        for k in range(n):
            at = (clip * n + k) * rows
            hid_ref[at : at + rows, :] = normalize(ref[k])[0].astype(BF16)
    pj_ref[...] = dot_nn(hid_ref[...], w_ref[...]).astype(BF16)
    lane = lax.broadcasted_iota(jnp.int32, (HALF, 128), 0) // HEAD_DIM
    head = lax.broadcasted_iota(jnp.int32, (HALF, 128), 1)
    gather_heads = jnp.where(lane == head, 1.0, 0.0).astype(BF16)
    lane = lax.broadcasted_iota(jnp.int32, (128, HALF), 1) // HEAD_DIM
    head = lax.broadcasted_iota(jnp.int32, (128, HALF), 0)
    spread_heads = jnp.where(lane == head, 1.0, 0.0).astype(BF16)
    for clip in range(2):
        cot_ref = (cot_own_ref, cot_other_ref)[clip]
        tout_ref = (tout_own_ref, tout_other_ref)[clip]

        def part(k, which):
            at = (clip * n + k) * rows
            return pj_ref[at : at + rows, which * HALF : (which + 1) * HALF]

        queries = [part(k, 0) for k in range(n)]
        keys_in = [part(k, 1) for k in range(n)]
        values_in = [part(k, 2) for k in range(n)]
        cots = [cot_ref[k] for k in range(n)]
        for f in range(n):
            for g in range(n):
                at = (f * n + g) * rows
                prod_ref[at : at + rows, :] = queries[f] * keys_in[g]
                at += n * n * rows
                prod_ref[at : at + rows, :] = cots[f] * values_in[g]
        score_ref[...] = dot_nn(prod_ref[...], gather_heads)
        count = (own_count_ref, other_count_ref)[clip][0]
        valid = [jnp.where(k < count, 1.0, 0.0) for k in range(n)]
        for f in range(n):
            raised, grad_probs = [], []
            for g in range(n):
                at = (f * n + g) * rows
                raised.append(jnp.exp(score_ref[at : at + rows, :] * SCALE) * valid[g])
                at += n * n * rows
                grad_probs.append(score_ref[at : at + rows, :])
            total = (raised[0] + raised[1]) + (raised[2] + raised[3])
            inverse = 1.0 / total
            probs = [r * inverse for r in raised]
            terms = [a * b for a, b in zip(grad_probs, probs)]
            delta = (terms[0] + terms[1]) + (terms[2] + terms[3])
            for g in range(n):
                at = (f * n + g) * rows
                weight_ref[at : at + rows, :] = probs[g].astype(BF16)
                at += n * n * rows
                weight_ref[at : at + rows, :] = (
                    probs[g] * (grad_probs[g] - delta) * SCALE
                ).astype(BF16)
        wide_ref[...] = dot_nn(weight_ref[...], spread_heads)

        def prob(f, g):
            at = (f * n + g) * rows
            return wide_ref[at : at + rows, :]

        def grad_score(f, g):
            at = (n * n + f * n + g) * rows
            return wide_ref[at : at + rows, :]

        for k in range(n):
            at = (clip * n + k) * rows
            out = sum(prob(k, g) * values_in[g].astype(F32) for g in range(n))
            tout_ref[k] = out.astype(BF16)
            grad_q = sum(grad_score(k, g) * keys_in[g].astype(F32) for g in range(n))
            grad_k = sum(grad_score(f, k) * queries[f].astype(F32) for f in range(n))
            grad_v = sum(prob(f, k) * cots[f].astype(F32) for f in range(n))
            gp_ref[at : at + rows, 0:HALF] = grad_q.astype(BF16)
            gp_ref[at : at + rows, HALF : 2 * HALF] = grad_k.astype(BF16)
            gp_ref[at : at + rows, 2 * HALF : 3 * HALF] = grad_v.astype(BF16)
    gh_other_ref[...] = dot_nt(gp_ref[n * rows :, :], w_ref[...]).astype(BF16)
    gh_own_ref[...] = dot_nt(gp_ref[: n * rows, :], w_ref[...])
    acc_ref[...] = dot_tn(hid_ref[...], gp_ref[:, : 2 * HALF])
    write_terms(True, info_ref, acc_ref, term_refs)
    v_term_ref[...] = dot_tn(hid_ref[...], gp_ref[:, 2 * HALF :])


def second_term_kernel(
    info_ref, v_ref, attn_own_ref, attn_other_ref, gx_own_ref, gx_other_ref, *refs
):
    acc_ref = refs[-1]
    acc_ref[:, :HALF] = v_ref[...]
    total = jnp.zeros((D, HALF), F32)
    for attn_ref, gx_ref in ((attn_own_ref, gx_own_ref), (attn_other_ref, gx_other_ref)):
        total = total + dot_tn(attn_ref[...], gx_ref[...])
    acc_ref[:, HALF:] = total
    write_terms(False, info_ref, acc_ref, refs[:-1])


def ring_sum_kernel(info_ref, *refs):
    n, half = 4, 2
    inputs, outputs = refs[:10], refs[10:]
    for side in range(2):
        keep, up, down, up_later, down_later = inputs[5 * side : 5 * side + 5]
        place = info_ref[3 - side]
        for j in range(n):
            if j < half:
                terms = (keep[j], down[half + j], up_later[j])
            else:
                terms = (keep[j], up[j], down_later[j - half])
            total = terms[0].astype(F32) + terms[1].astype(F32) + terms[2].astype(F32)
            total = total.astype(BF16)
            for k in range(n):

                @pl.when(lax.rem(place + k, n) == j)
                def _(k=k):
                    outputs[4 * side + k][...] = total


def share_kernel(info_ref, *refs):
    keep_ref, send_ref, share_ref = refs[8:]
    for side in range(2):
        part = refs[4 * side][...].astype(F32)
        for ref in refs[4 * side + 1 : 4 * side + 4]:
            part = part + ref[...].astype(F32)
        share_ref[:, side * D : (side + 1) * D] = part
    per = keep_ref.shape[0]
    first, second = share_ref[:per, :], share_ref[per:, :]
    is_first = info_ref[1] == 0
    keep_ref[...] = jnp.where(is_first, first, second).astype(BF16)
    send_ref[...] = jnp.where(is_first, second, first).astype(BF16)


def final_kernel(factor, info_ref, a_ref, a_got_ref, b_ref, b_got_ref, out_ref, qkv_ref):
    mine = (a_ref[...].astype(F32) + a_got_ref[...].astype(F32)) * factor
    partner = (b_ref[...].astype(F32) + b_got_ref[...].astype(F32)) * factor
    is_first = info_ref[1] == 0
    left = jnp.where(is_first, mine, partner)
    right = jnp.where(is_first, partner, mine)
    for i in range(3):
        columns = slice(i * HALF, (i + 1) * HALF)
        qkv_ref[:, i * D : i * D + HALF] = left[:, columns]
        qkv_ref[:, i * D + HALF : (i + 1) * D] = right[:, columns]
    out_ref[:, :HALF] = left[:, 3 * HALF :]
    out_ref[:, HALF:] = right[:, 3 * HALF :]


def add_kernel(count, *refs):
    for i in range(len(refs) // (count + 1)):
        total = refs[i * count][...].astype(F32)
        for ref in refs[i * count + 1 : (i + 1) * count]:
            total = total + ref[...].astype(F32)
        out_ref = refs[-(len(refs) // (count + 1)) + i]
        out_ref[...] = total.astype(out_ref.dtype)


def norm_back_kernel(
    info_ref, resid_ref, own_ref, other_ref, pair_ref, out_ref, mine_ref, theirs_ref
):
    is_first = info_ref[1] == 0
    for k in range(resid_ref.shape[0]):
        rows = slice(k * TILE, (k + 1) * TILE)
        grad_hidden = own_ref[rows, :] + other_ref[rows, :].astype(F32)
        normed, rstd_vals = normalize(resid_ref[k])
        inner = grad_hidden - jnp.mean(grad_hidden, axis=-1, keepdims=True)
        inner = inner - normed * jnp.mean(grad_hidden * normed, axis=-1, keepdims=True)
        norm_back = (rstd_vals * inner).astype(BF16).astype(F32)
        out_ref[k] = (pair_ref[k, :, :D].astype(F32) + norm_back).astype(BF16)
        first, second = out_ref[k, :, :HALF], out_ref[k, :, HALF:]
        mine_ref[rows, :] = jnp.where(is_first, first, second)
        theirs_ref[rows, :] = jnp.where(is_first, second, first)


def per_device(
    inputs, qkv_spatial, tile_list, tile_count, frame_count, w_out, w_qkv, cot_y, cot_out
):
    seq_count = lax.axis_size("seq")
    fsdp_count = lax.axis_size("fsdp")
    tok_frame = inputs.shape[2]
    place = lax.axis_index("seq")
    core = lax.axis_index("fsdp") % 2
    chip = lax.axis_index("fsdp") // 2
    info = jnp.stack([place, core, chip // 4, chip % 4]).astype(jnp.int32)
    pairs = [(i, i ^ 1) for i in range(fsdp_count)]
    groups = [list(range(c, fsdp_count, 2)) for c in range(2)]
    first_core = core == 0

    def swap(values):
        return lax.ppermute(values, "fsdp", pairs)

    def over_seq(blocks):
        return lax.all_to_all(blocks, "seq", split_axis=0, concat_axis=0, tiled=True)

    def along(axis, values, k):
        def moved(i):
            x, z, c = i // 8, i // 2 % 4, i % 2
            x, z = ((x + k) % 4, z) if axis == 0 else (x, (z + k) % 4)
            return x * 8 + z * 2 + c

        return lax.ppermute(values, "fsdp", [(i, moved(i)) for i in range(fsdp_count)])

    def after(values, earlier):
        return lax.optimization_barrier((values, earlier))[0]

    def mirror(values, which):
        return lax.ppermute(
            values, "seq", [(i, i ^ 1 if which == 0 else 3 - i) for i in range(seq_count)]
        )

    def to_chips(blocks):
        return lax.all_to_all(
            blocks, "fsdp", split_axis=0, concat_axis=0, tiled=True, axis_index_groups=groups
        )

    def mine_theirs(first, second):
        return jnp.where(first_core, first, second), jnp.where(first_core, second, first)

    def shaped(shape, dtype=BF16):
        return jax.ShapeDtypeStruct(shape, dtype)

    def half_columns(c):
        cuts = [w_qkv[:, i * D + c * HALF : i * D + (c + 1) * HALF] for i in range(3)]
        return jnp.concatenate(cuts + [w_out[:, c * HALF : (c + 1) * HALF]], axis=1)

    mine, theirs = mine_theirs(half_columns(0), half_columns(1))
    got = swap(theirs)
    top, bottom = mine_theirs(mine, got)
    chip_rows = jnp.concatenate([top, bottom], axis=0)
    half_qkv = lax.all_gather(
        chip_rows[:, : 3 * HALF], "fsdp", axis=0, tiled=True, axis_index_groups=groups
    )
    cot_mine, cot_theirs = mine_theirs(cot_out[0][..., :HALF], cot_out[0][..., HALF:])
    cot_other = swap(cot_theirs)
    other_count = swap(frame_count)

    qkv = qkv_spatial.reshape(tok_frame, 3 * D)
    lists = tile_list.reshape(-1, LIST_LEN)
    counts = tile_count.reshape(-1)
    mask_scratch = pltpu.VMEM((tok_frame, tok_frame), F32)
    attn = call(
        spatial_forward_kernel,
        shaped((tok_frame, D)),
        (lists, counts, qkv),
        [SMEM, SMEM, VMEM],
        [mask_scratch],
        flops=4 * 10**9,
        nbytes=3 * 10**6,
    )
    chips = fsdp_count // 2
    out_rows = jnp.broadcast_to(chip_rows[None, :, 3 * HALF :], (chips, 2 * w_out.shape[0], HALF))
    half_out = to_chips(after(out_rows, (attn, cot_mine, cot_theirs)))
    other_out = swap(half_out).reshape(D, HALF)
    half_out = half_out.reshape(D, HALF)
    resid = call(
        resid_kernel,
        shaped((tok_frame, D)),
        (info, inputs.reshape(tok_frame, D), attn, half_out, other_out),
        [SMEM, VMEM, VMEM, VMEM, VMEM],
        [pltpu.VMEM((D, D), BF16)],
        limit=16,
        flops=2 * 10**9,
        nbytes=4 * 10**6,
    )
    own = over_seq(resid.reshape(seq_count, TILE, D))
    other = swap(own)
    pair = jnp.concatenate([cot_y.reshape(tok_frame, D), attn], axis=1)
    pair = over_seq(after(pair, own).reshape(seq_count, TILE, 2 * D))
    attn_own = pair[..., D:].reshape(tok_frame, D)
    attn_other = swap(attn_own)
    wide = 2 * seq_count * seq_count * TILE
    rows = seq_count * TILE
    blocks = [shaped((size, CHIP_ROWS, D)) for size in (4, 4, 2, 2, 4)]
    tout_own, tout_other, gh_own, gh_other, v_term, *first_terms = call(
        temporal_kernel,
        [
            shaped((seq_count, TILE, HALF)),
            shaped((seq_count, TILE, HALF)),
            shaped((rows, D), F32),
            shaped((rows, D)),
            shaped((D, HALF), F32),
        ]
        + blocks,
        (info, frame_count, other_count, own, other, half_qkv, cot_mine, cot_other),
        [SMEM] * 3 + [VMEM] * 5,
        [
            pltpu.VMEM((2 * rows, D), BF16),
            pltpu.VMEM((2 * rows, 3 * HALF), BF16),
            pltpu.VMEM((D, D), F32),
            pltpu.VMEM((2 * rows, 3 * HALF), BF16),
            pltpu.VMEM((wide, HALF), BF16),
            pltpu.VMEM((wide, 128), F32),
            pltpu.VMEM((wide, 128), BF16),
            pltpu.VMEM((wide, HALF), F32),
        ],
        limit=58,
        flops=10**10,
        nbytes=10**7,
    )
    gh_got = swap(gh_other)
    grad_x, gx_mine, gx_theirs = call(
        norm_back_kernel,
        [shaped((seq_count, TILE, D))] + [shaped((rows, HALF))] * 2,
        (info, own, gh_own, gh_got, pair),
        [SMEM] + [VMEM] * 4,
        flops=10**8,
        nbytes=3 * 10**6,
    )
    gx_got = swap(gx_theirs)
    second_terms = call(
        second_term_kernel,
        blocks,
        (info, v_term, attn_own, attn_other, gx_mine, gx_got),
        [SMEM] + [VMEM] * 5,
        [pltpu.VMEM((D, D), F32)],
        limit=24,
        flops=2 * 10**9,
        nbytes=5 * 10**6,
    )
    grad_x = over_seq(after(grad_x, second_terms)).reshape(tok_frame, D)
    first_terms = after(first_terms, second_terms)
    sums = []
    for side, terms in enumerate((first_terms, second_terms)):
        up, down, up_later, down_later, keep = terms
        up, down = along(side, up, 1), along(side, down, -1)
        up_later = (up_later.astype(F32) + up[:2].astype(F32)).astype(BF16)
        down_later = (down_later.astype(F32) + down[:2].astype(F32)).astype(BF16)
        sums.append([keep, up, down, up_later, down_later])
    tout_got = swap(after(tout_other, sums))
    grad_qkv, tout, grad_x = call(
        spatial_back_kernel,
        [shaped((tok_frame, 3 * D)), shaped((seq_count, TILE, D)), shaped((tok_frame, D))],
        (info, lists, counts, qkv, after(grad_x, sums), half_out, other_out, tout_own, tout_got),
        [SMEM] * 3 + [VMEM] * 6,
        [mask_scratch, pltpu.VMEM((tok_frame, D), BF16), pltpu.VMEM((D, D), BF16)],
        limit=56,
        flops=10**10,
        nbytes=7 * 10**6,
    )
    for side in range(2):
        sums[side][3:] = [along(side, sums[side][3], 1), along(side, sums[side][4], -1)]
    chip_share = shaped((CHIP_ROWS, D))
    parts = call(
        ring_sum_kernel,
        [chip_share] * 8,
        after((info, *sums[0], *sums[1]), grad_qkv),
        [SMEM] + [VMEM] * 10,
        flops=10**7,
        nbytes=10**7,
    )
    adds = []
    for side in range(2):
        adds += [parts[4 * side]]
        adds += [along(1 - side, parts[4 * side + k], k) for k in (1, 2, 3)]
    per = w_out.shape[0]
    keep, send = call(
        share_kernel,
        [shaped((per, 4 * HALF))] * 2,
        (info, *adds),
        [SMEM] + [VMEM] * 8,
        [pltpu.VMEM((CHIP_ROWS, 4 * HALF), F32)],
        nbytes=3 * 10**6,
    )
    got = swap(send)
    keep, got = call(
        functools.partial(add_kernel, 2),
        [shaped((per, 4 * HALF))] * 2,
        (keep, mirror(keep, 0), got, mirror(got, 1)),
        [VMEM] * 4,
        nbytes=10**6,
    )
    grad_w_out, grad_w_qkv = call(
        functools.partial(final_kernel, 1.0 / math.sqrt(fsdp_count * seq_count * tok_frame)),
        [shaped((per, D), F32), shaped((per, 3 * D), F32)],
        (info, keep, mirror(keep, 1), got, mirror(got, 0)),
        [SMEM] + [VMEM] * 4,
        nbytes=10**6,
    )
    return (
        resid.reshape(inputs.shape),
        tout[None],
        grad_x.reshape(inputs.shape),
        grad_qkv.reshape(qkv_spatial.shape),
        grad_w_out,
        grad_w_qkv,
    )


def solution(mesh):
    placed = (
        P("fsdp", "seq", None, None),
        P("fsdp", "seq", None, None),
        P("fsdp", "seq", None, None),
        P("fsdp", "seq", None),
        P("fsdp"),
        P("fsdp", None),
        P("fsdp", None),
        P("fsdp", "seq", None, None),
        P("fsdp", None, "seq", None),
    )
    return jax.shard_map(
        per_device,
        mesh=mesh,
        in_specs=placed,
        out_specs=(
            P("fsdp", "seq", None, None),
            P("fsdp", None, "seq", None),
            P("fsdp", "seq", None, None),
            P("fsdp", "seq", None, None),
            P("fsdp", None),
            P("fsdp", None),
        ),
        check_vma=False,
    )
```
